128 devices in a mesh: ctx: 64 (over x, y, z), head: 2 (over core).
Axes of the slice: x: 4, y: 4, z: 4, core: 2. Of those that a mesh axis runs over, the one named last changes fastest.
Arguments:
- queries: bfloat16 [32768, 32, 128], P(('ctx', 'head')), may hold values from -112 to 112
- key_states: bfloat16 [32768, 8, 128], P(('ctx', 'head')), may hold values from -4 to 4
- value_states: bfloat16 [32768, 8, 128], P(('ctx', 'head')), may hold values from -5 to 5
- column_blocks: int32 [32, 4], replicated, may hold values from 0 to 255, as said below
- column_count: int32 [32], replicated, may hold values from 1 to 4
- slash_offsets: int32 [32, 16], replicated, may hold values from 0 to 255, as said below
- slash_count: int32 [32], replicated, may hold values from 1 to 16
Outputs:
- attended: bfloat16 [32768, 32, 128], P(('ctx', 'head'))
The draws below stay inside these ranges and needn't reach their ends.
Inputs may be any that keep to these rules, and one draw needn't show every extreme that they name: `column_blocks`: the 4 entries of a head's row are distinct block numbers. `slash_offsets`: the entries of a head's row are distinct and the first is 0.
All inputs are finite; a program needn't handle non-finite values.
Results may differ from the reference program's by a relative error of at most 0.003.
Values may be sent and summed in bfloat16 or wider, within the bound.
A program may use at most 128 MiB of HBM per device.

```python
import math
import jax
import jax.numpy as jnp
from jax import lax

HEADS = 32
KV_HEADS = 8
HDIM = 128
BLOCK = 128
VSLOTS = 4
SSLOTS = 16
BAND = 256
TOKENS = 32768
BLOCKS = 256


def shared_keys(key):
    return jax.random.truncated_normal(jax.random.fold_in(key, 11), -4.0, 4.0, (TOKENS, KV_HEADS, HDIM), jnp.float32)


def chosen_head(key):
    return jax.random.randint(jax.random.fold_in(key, 13), (), 0, HEADS)


def first_blocks(one_key):
    return jax.random.permutation(one_key, BLOCKS)[:VSLOTS]


def first_offsets(one_key):
    return jax.random.permutation(one_key, BAND - 1)[:SSLOTS - 1] + 1


def draw_key_states(key, part):
    base = shared_keys(key)
    return base.astype(jnp.bfloat16)


def draw_queries(key, part):
    key = jax.random.fold_in(key, 2)
    fresh_key = jax.random.fold_in(key, 0)
    fresh = jax.random.truncated_normal(fresh_key, -4.0, 4.0, (TOKENS, HEADS, HDIM), jnp.float32)
    return fresh.astype(jnp.bfloat16)


def draw_column_blocks(key, part):
    target = chosen_head(key)
    key = jax.random.fold_in(key, 3)
    listed = jax.vmap(first_blocks)(jax.random.split(key, HEADS)).astype(jnp.int32)
    last_block = BLOCKS - 1
    swapped = jnp.where(listed == last_block, listed[:, :1], listed)
    swapped = swapped.at[:, 0].set(last_block)
    swapped = jnp.where(swapped == 0, swapped[:, 1:2], swapped)
    swapped = swapped.at[:, 1].set(0)
    return jnp.where(jnp.arange(HEADS)[:, None] == target, swapped, listed).astype(jnp.int32)


def draw_column_count(key, part):
    target = chosen_head(key)
    key = jax.random.fold_in(key, 4)
    counts = jax.random.randint(key, (HEADS,), 1, VSLOTS + 1)
    return jnp.where(jnp.arange(HEADS) == target, VSLOTS, counts).astype(jnp.int32)


def draw_slash_offsets(key, part):
    target = chosen_head(key)
    key = jax.random.fold_in(key, 5)
    listed = jax.vmap(first_offsets)(jax.random.split(key, HEADS)).astype(jnp.int32)
    last_offset = BAND - 1
    swapped = jnp.where(listed == last_offset, listed[:, :1], listed)
    swapped = swapped.at[:, 0].set(last_offset)
    chosen_rows = jnp.where(jnp.arange(HEADS)[:, None] == target, swapped, listed)
    return jnp.concatenate([jnp.zeros((HEADS, 1), jnp.int32), chosen_rows], axis=1).astype(jnp.int32)


def draw_slash_count(key, part):
    target = chosen_head(key)
    key = jax.random.fold_in(key, 6)
    counts = jax.random.randint(key, (HEADS,), 1, SSLOTS + 1)
    return jnp.where(jnp.arange(HEADS) == target, SSLOTS, counts).astype(jnp.int32)


def levels(stream_key, extent, shards, least, high):
    def one(dim, shards_of):
        draws = jax.random.uniform(jax.random.fold_in(jax.random.fold_in(stream_key, 6), dim), (shards_of,), jnp.float32, least / len(shards), high / len(shards))
        return jnp.repeat(jnp.exp(draws), extent[dim] // shards_of).reshape((-1,) + (1,) * (len(extent) - dim - 1))

    factor_of = one(*shards[0])
    for cut in shards[1:]:
        factor_of = factor_of * one(*cut)
    return factor_of


def gaussian(rng, extent, scale, reach, cuts=(), kind=jnp.bfloat16):
    values = jax.random.normal(rng, extent, jnp.float32) * scale
    if len(cuts) > 0:
        values = levels(rng, extent, cuts, -0.22, 0.18) * values
    return jnp.clip(values, min=-reach, max=reach).astype(kind)


def setup_inputs(seed: int = 0) -> dict:
    arg_keys = jax.random.split(jax.random.key(seed), 8)
    queries = draw_queries(jax.random.fold_in(arg_keys[7], 71), 0)
    key_states = draw_key_states(jax.random.fold_in(arg_keys[7], 71), 0)
    value_states = gaussian(arg_keys[2], (TOKENS, KV_HEADS, HDIM), 1.0, 5.0, ((0, 128),))
    column_blocks = draw_column_blocks(jax.random.fold_in(arg_keys[7], 71), 0)
    column_count = draw_column_count(jax.random.fold_in(arg_keys[7], 71), 0)
    slash_offsets = draw_slash_offsets(jax.random.fold_in(arg_keys[7], 71), 0)
    slash_count = draw_slash_count(jax.random.fold_in(arg_keys[7], 71), 0)
    return {"queries": queries, "key_states": key_states, "value_states": value_states, "column_blocks": column_blocks, "column_count": column_count, "slash_offsets": slash_offsets, "slash_count": slash_count}


def reference(queries, key_states, value_states, column_blocks, column_count, slash_offsets, slash_count):
    total_rows = queries.shape[0]
    per_group = HEADS // KV_HEADS
    scale_factor = 1.0 / math.sqrt(HDIM)
    slot_live = jnp.arange(VSLOTS, dtype=jnp.int32)[None, :] < column_count[:, None]
    offset_live = jnp.arange(SSLOTS, dtype=jnp.int32)[None, :] < slash_count[:, None]
    diagonal_table = jnp.any((jnp.arange(BAND, dtype=jnp.int32)[None, :, None] == slash_offsets[:, None, :]) & offset_live[:, None, :], axis=2)
    column_pos = (column_blocks[:, :, None] * BLOCK + jnp.arange(BLOCK, dtype=jnp.int32)[None, None, :]).reshape(HEADS, VSLOTS * BLOCK)
    column_live = jnp.repeat(slot_live, BLOCK, axis=1)
    head_owner = jnp.arange(HEADS, dtype=jnp.int32) // per_group
    column_keys = key_states[column_pos, head_owner[:, None]].astype(jnp.float32)
    column_values = value_states[column_pos, head_owner[:, None]].astype(jnp.float32)
    padded_keys = jnp.concatenate([jnp.zeros((BAND, KV_HEADS, HDIM), key_states.dtype), key_states], axis=0)
    padded_values = jnp.concatenate([jnp.zeros((BAND, KV_HEADS, HDIM), value_states.dtype), value_states], axis=0)
    rows_block = min(512, total_rows)

    def one_block(block_index):
        low_row = (block_index * rows_block).astype(jnp.int32)
        query_rows = lax.dynamic_slice_in_dim(queries, low_row, rows_block, 0).astype(jnp.float32)
        window_keys = lax.dynamic_slice_in_dim(padded_keys, low_row, BAND + rows_block, 0)[:, head_owner].astype(jnp.float32)
        window_values = lax.dynamic_slice_in_dim(padded_values, low_row, BAND + rows_block, 0)[:, head_owner].astype(jnp.float32)
        query_pos = low_row + jnp.arange(rows_block, dtype=jnp.int32)
        window_pos = low_row - BAND + jnp.arange(BAND + rows_block, dtype=jnp.int32)
        gap_rows = query_pos[:, None] - window_pos[None, :]
        in_range = (gap_rows >= 0) & (gap_rows < BAND)
        on_slash = jnp.take(diagonal_table, jnp.clip(gap_rows, 0, BAND - 1), axis=1) & in_range[None]
        in_columns = jnp.any(((window_pos // BLOCK)[None, :, None] == column_blocks[:, None, :]) & slot_live[:, None, :], axis=2)
        band_ok = on_slash & (window_pos >= 0)[None, None, :] & jnp.logical_not(in_columns)[:, None, :]
        column_ok = column_live[:, None, :] & (column_pos[:, None, :] <= query_pos[None, :, None])
        band_scores = jnp.einsum('qhd,khd->hqk', query_rows, window_keys) * scale_factor
        column_scores = jnp.einsum('qhd,hkd->hqk', query_rows, column_keys) * scale_factor
        band_top = lax.optimization_barrier(jnp.max(jnp.where(band_ok, band_scores, -jnp.inf), axis=2, keepdims=True))
        column_top = lax.optimization_barrier(jnp.max(jnp.where(column_ok, column_scores, -jnp.inf), axis=2, keepdims=True))
        row_top = jnp.maximum(band_top, column_top)
        band_weights = jnp.where(band_ok, jnp.exp(band_scores - row_top), 0.0)
        column_weights = jnp.where(column_ok, jnp.exp(column_scores - row_top), 0.0)
        row_total = lax.optimization_barrier(jnp.sum(band_weights, axis=2)) + lax.optimization_barrier(jnp.sum(column_weights, axis=2))
        band_rounded = band_weights.astype(jnp.bfloat16).astype(jnp.float32)
        column_rounded = column_weights.astype(jnp.bfloat16).astype(jnp.float32)
        mixed = jnp.einsum('hqk,khd->qhd', band_rounded, window_values) + jnp.einsum('hqk,hkd->qhd', column_rounded, column_values)
        return (mixed / row_total.T[:, :, None]).astype(jnp.bfloat16)
    blocks_out = lax.map(one_block, jnp.arange(total_rows // rows_block, dtype=jnp.int32))
    return blocks_out.reshape(total_rows, HEADS, HDIM)
```

```python
import functools
import math

import jax
import jax.numpy as jnp
from jax import lax
from jax.experimental import pallas as pl
from jax.experimental.pallas import tpu as pltpu
from jax.sharding import PartitionSpec as P

HEADS = 32
KV_HEADS = 8
HDIM = 128
BLOCK = 128
VSLOTS = 4
SSLOTS = 16
BAND = 256
CTX = 64
SIDE = 4
NEG = -1e30
MESH = pl.DeviceIdType.MESH
BF16 = jnp.bfloat16


def gather_kernel(
    Q, R, sel_ref, own_ref, kv_ref, g_ref, halo_ref, send, recv, home,
    s1_send, s1_recv, st_send, st_recv, sib_send, sib_recv, loc_sem, halo_send, halo_recv,
):
    c = lax.axis_index("ctx")
    k = lax.axis_index("head")
    coords = (c // 16, (c // 4) % 4, c % 4)
    x, y, z = coords
    barrier = pltpu.get_barrier_semaphore()

    @pl.loop(1, CTX)
    def _(d):
        pl.semaphore_signal(barrier, inc=1, device_id={"ctx": (c + d) % CTX}, device_id_type=MESH)

    pl.semaphore_signal(barrier, inc=1, device_id={"head": 1 - k}, device_id_type=MESH)

    @pl.when(k == 0)
    def _():
        pl.semaphore_signal(
            barrier, inc=1, device_id={"ctx": (c + CTX - 1) % CTX, "head": 1}, device_id_type=MESH
        )

    for r in range(R):
        for u in range(8):
            send[r, u] = kv_ref[sel_ref[r * 8 + u]]
    pl.semaphore_wait(barrier, CTX + k)

    @pl.loop(1, CTX)
    def _(d):
        p = (c + d) % CTX
        for r in range(R):
            pltpu.make_async_remote_copy(
                src_ref=send.at[r, p // 8, pl.ds((p % 8) * 16, 16)],
                dst_ref=recv.at[r, c],
                send_sem=s1_send,
                recv_sem=s1_recv,
                device_id={"ctx": p},
                device_id_type=MESH,
            ).start()

    halo = pltpu.make_async_remote_copy(
        src_ref=kv_ref,
        dst_ref=halo_ref,
        send_sem=halo_send,
        recv_sem=halo_recv,
        device_id={"ctx": (c + k) % CTX, "head": 1 - k},
        device_id_type=MESH,
    )
    halo.start()
    for r in range(R):
        recv[r, c] = send[r, c // 8, pl.ds((c % 8) * 16, 16)]
    others = recv.at[:, pl.ds(0, CTX - 1)]
    pltpu.make_async_copy(others, others, s1_recv).wait()
    for q in range(Q):
        home[q] = recv[q % R, own_ref[q]]
    own_copy = pltpu.make_async_copy(home, g_ref.at[k, :, x, y, z], loc_sem)
    own_copy.start()
    own_copy.wait()

    def along(axis, delta):
        there = list(coords)
        there[axis] = (there[axis] + delta) % SIDE
        return {"ctx": there[0] * 16 + there[1] * 4 + there[2]}

    bounds = [0, (Q + 2) // 3, (2 * Q + 2) // 3, Q]

    def view(t, s, pos, half=None):
        index = [None] * 3
        for i in range(3):
            axis = (t + i) % 3
            index[axis] = slice(None) if i < s else pos if i == s else coords[axis]
        lanes = slice(None) if half is None else pl.ds(half * 128, 128)
        rows = pl.ds(bounds[t], bounds[t + 1] - bounds[t])
        return g_ref.at[k, rows, index[0], index[1], index[2], :, lanes]

    def push(ref, t, s, i, device):
        copy = pltpu.make_async_remote_copy(
            src_ref=ref, dst_ref=ref, send_sem=st_send.at[t, s, i], recv_sem=st_recv.at[t, s, i],
            device_id=device, device_id_type=MESH,
        )
        copy.start()
        return copy

    pending = []
    across = []

    def to_sibling(ref):
        i = len(across)
        copy = pltpu.make_async_remote_copy(
            src_ref=ref, dst_ref=ref, send_sem=sib_send.at[i], recv_sem=sib_recv.at[i],
            device_id={"head": 1 - k}, device_id_type=MESH,
        )
        copy.start()
        across.append(copy)

    first = {}

    def begin(t, s):
        axis = (t + s) % 3
        own = view(t, s, coords[axis])
        first[t] = (push(own, t, s, 0, along(axis, 1)), push(own, t, s, 1, along(axis, -1)))

    def middle(t, s):
        axis = (t + s) % 3
        me = coords[axis]
        left, right = (me + 3) % 4, (me + 1) % 4
        to_right, to_left = first[t]
        to_right.wait_recv()
        on_right = push(view(t, s, left, 0), t, s, 2, along(axis, 1))
        to_left.wait_recv()
        on_left = push(view(t, s, right, 1), t, s, 3, along(axis, -1))
        if s == 2:
            to_sibling(view(t, s, left))
            to_sibling(view(t, s, right))
        pending.extend([to_right, to_left, on_right, on_left])
        return on_right, on_left

    def end(t, s, on_right, on_left):
        axis = (t + s) % 3
        on_right.wait_recv()
        on_left.wait_recv()
        if s == 2:
            to_sibling(view(t, s, (coords[axis] + 2) % 4))

    for t in range(3):
        begin(t, 0)
    for s in range(3):
        passed = [middle(t, s) for t in range(3)]
        for t in range(3):
            end(t, s, *passed[t])
            if s < 2:
                begin(t, s + 1)
            if s == 1:
                to_sibling(view(t, 2, coords[(t + 2) % 3]))
    halo.wait_recv()
    for copy in across:
        copy.wait_recv()
    for copy in pending:
        copy.wait_send()
    for copy in across:
        copy.wait_send()
    halo.wait_send()
    pltpu.make_async_copy(others, others, s1_send).wait()


def gather_pairs(sel, own, kv, Q, R, collective_id):
    return pl.pallas_call(
        functools.partial(gather_kernel, Q, R),
        out_shape=(
            jax.ShapeDtypeStruct((2, Q, 4, 4, 4, 16, 256), BF16),
            jax.ShapeDtypeStruct((16, 128, 256), BF16),
        ),
        in_specs=[
            pl.BlockSpec(memory_space=pltpu.SMEM),
            pl.BlockSpec(memory_space=pltpu.SMEM),
            pl.BlockSpec(memory_space=pltpu.VMEM),
        ],
        out_specs=(pl.BlockSpec(memory_space=pl.ANY), pl.BlockSpec(memory_space=pl.ANY)),
        scratch_shapes=[
            pltpu.VMEM((R, 8, 128, 256), BF16),
            pltpu.VMEM((R, CTX, 16, 256), BF16),
            pltpu.VMEM((Q, 16, 256), BF16),
            pltpu.SemaphoreType.DMA(()),
            pltpu.SemaphoreType.DMA(()),
            pltpu.SemaphoreType.DMA((3, 3, 4)),
            pltpu.SemaphoreType.DMA((3, 3, 4)),
            pltpu.SemaphoreType.DMA((12,)),
            pltpu.SemaphoreType.DMA((12,)),
            pltpu.SemaphoreType.DMA(()),
            pltpu.SemaphoreType.DMA(()),
            pltpu.SemaphoreType.DMA(()),
        ],
        compiler_params=pltpu.CompilerParams(
            collective_id=collective_id, has_side_effects=True, vmem_limit_bytes=32 * 2**20
        ),
    )(sel, own, kv)


LOG2E = 1.4426950408889634
GROUPS = 2


def attend_kernel(
    slot_ref, code_ref, q_ref, kv_ref, halo_ref, base_ref, cbias_ref, g_ref, o_ref, cols, sems
):
    step = pl.program_id(0)
    steps = pl.num_programs(0)
    per_step = GROUPS * 4 * VSLOTS

    def fetch(at, slot):
        for i in range(per_step):
            pltpu.make_async_copy(
                g_ref.at[slot_ref[at * per_step + i]],
                cols.at[slot, i // VSLOTS, pl.ds((i % VSLOTS) * BLOCK, BLOCK)],
                sems.at[slot],
            ).start()

    @pl.when(step == 0)
    def _():
        fetch(0, 0)

    @pl.when(step + 1 < steps)
    def _():
        fetch(step + 1, (step + 1) % 2)

    now = step % 2
    q8 = jnp.swapaxes(q_ref[...], 0, 1)
    row = lax.broadcasted_iota(jnp.int32, (BLOCK, BLOCK), 0)
    col = lax.broadcasted_iota(jnp.int32, (BLOCK, BLOCK), 1)
    triangle = jnp.where(col <= row, 0.0, NEG)
    factor = LOG2E / math.sqrt(HDIM)
    nt = (((1,), (1,)), ((), ()))
    pltpu.make_async_copy(cols.at[now], cols.at[now], sems.at[now]).wait()
    outs = [[None, None] for _ in range(GROUPS * 4)]
    for group in range(GROUPS):
        window = jnp.concatenate([halo_ref[group], kv_ref[group]], axis=0)
        tables = []
        for hh in range(4):
            line = base_ref[pl.ds(group * 4 + hh, 1), :]
            tables.append(
                pltpu.roll(
                    jnp.broadcast_to(line, (BLOCK, 3 * BLOCK)), 0, 1, stride=1, stride_axis=0
                )
            )
        for j in range(2):
            keys = window[j * BLOCK : j * BLOCK + 3 * BLOCK, :HDIM]
            values = window[j * BLOCK : j * BLOCK + 3 * BLOCK, HDIM:]
            rows = q8[group * 4 : group * 4 + 4, j * BLOCK : (j + 1) * BLOCK]
            band = lax.dot_general(
                rows.reshape(4 * BLOCK, HDIM), keys, nt, preferred_element_type=jnp.float32
            )
            for hh in range(4):
                head = group * 4 + hh
                pieces = []
                for w in range(3):
                    code = code_ref[(step * GROUPS * 4 + head) * 4 + j + w]
                    other = triangle if w == 2 else jnp.zeros_like(triangle)
                    bias = jnp.where(
                        code == 0, tables[hh][:, w * BLOCK : (w + 1) * BLOCK], other
                    )
                    if w < 2:
                        bias = jnp.where(code == 2, NEG, bias)
                    pieces.append(bias)
                bscore = band[hh * BLOCK : (hh + 1) * BLOCK] + jnp.concatenate(pieces, axis=1)
                ck = cols[now, head, :, :HDIM]
                cv = cols[now, head, :, HDIM:]
                cscore = lax.dot_general(
                    rows[hh], ck, nt, preferred_element_type=jnp.float32
                ) + cbias_ref[pl.ds(head * 2 + j, 1), :]
                top = jnp.maximum(
                    jnp.max(bscore, axis=1, keepdims=True), jnp.max(cscore, axis=1, keepdims=True)
                )
                bw = jnp.exp2((bscore - top) * factor)
                cw = jnp.exp2((cscore - top) * factor)
                total = jnp.sum(bw, axis=1, keepdims=True) + jnp.sum(cw, axis=1, keepdims=True)
                mixed = jnp.dot(bw.astype(BF16), values, preferred_element_type=jnp.float32)
                mixed += jnp.dot(cw.astype(BF16), cv, preferred_element_type=jnp.float32)
                outs[head][j] = (mixed / total).astype(BF16)
    stacked = jnp.stack([jnp.concatenate(pair, axis=0) for pair in outs], axis=0)
    o_ref[...] = jnp.swapaxes(stacked, 0, 1)


def attend(slots, codes, queries, kv, halo, base, cbias, pairs):
    steps = KV_HEADS // GROUPS
    heads = GROUPS * 4
    tokens = queries.shape[0]
    return pl.pallas_call(
        attend_kernel,
        grid=(steps,),
        out_shape=jax.ShapeDtypeStruct(queries.shape, BF16),
        in_specs=[
            pl.BlockSpec(memory_space=pltpu.SMEM),
            pl.BlockSpec(memory_space=pltpu.SMEM),
            pl.BlockSpec((tokens, heads, HDIM), lambda i: (0, i, 0)),
            pl.BlockSpec((GROUPS, 256, 256), lambda i: (i, 0, 0)),
            pl.BlockSpec((GROUPS, 256, 256), lambda i: (i, 0, 0)),
            pl.BlockSpec((heads, 384), lambda i: (i, 0)),
            pl.BlockSpec((heads * 2, 512), lambda i: (i, 0)),
            pl.BlockSpec(memory_space=pl.ANY),
        ],
        out_specs=pl.BlockSpec((tokens, heads, HDIM), lambda i: (0, i, 0)),
        scratch_shapes=[
            pltpu.VMEM((2, heads, VSLOTS * BLOCK, 2 * HDIM), BF16),
            pltpu.SemaphoreType.DMA((2,)),
        ],
        compiler_params=pltpu.CompilerParams(vmem_limit_bytes=48 * 2**20),
    )(slots, codes, queries, kv, halo, base, cbias, pairs)


def body(queries, key_states, value_states, column_blocks, column_count, slash_offsets, slash_count):
    c = lax.axis_index("ctx")
    k = lax.axis_index("head")
    kv = jnp.swapaxes(jnp.concatenate([key_states, value_states], axis=2), 0, 1)

    block = column_blocks.reshape(HEADS * VSLOTS)
    index = jnp.arange(HEADS * VSLOTS, dtype=jnp.int32)
    live = (jnp.arange(VSLOTS, dtype=jnp.int32)[None] < column_count[:, None]).reshape(-1)
    group = index // (4 * VSLOTS)
    pid = block * KV_HEADS + group
    core = (block // 2) % 2
    device = block // 2
    first = live & ~jnp.any(
        (pid[:, None] == pid[None]) & live[None] & (index[None] < index[:, None]), axis=1
    )
    same_core = first[None] & (core[None] == core[:, None])
    rank = jnp.sum(same_core & (pid[None] < pid[:, None]), axis=1, dtype=jnp.int32)
    most = jnp.max(jnp.sum(same_core & live[:, None], axis=1, dtype=jnp.int32))
    load = jnp.max(
        jnp.sum(first[None] & live[:, None] & (device[None] == device[:, None]), axis=1, dtype=jnp.int32)
    )

    olive = jnp.arange(SSLOTS, dtype=jnp.int32)[None] < slash_count[:, None]
    spot = jnp.arange(3 * BLOCK, dtype=jnp.int32)
    seen = jnp.any(
        (2 * BLOCK - spot[None, :, None] == slash_offsets[:, None, :]) & olive[:, None, :], axis=2
    )
    base = jnp.where(seen, 0.0, NEG).astype(jnp.float32)
    q0 = (c * 2 + k) * 2
    near = q0 - 2 + jnp.arange(4, dtype=jnp.int32)
    live4 = live.reshape(HEADS, VSLOTS)
    listed = jnp.any((column_blocks[:, None, :] == near[None, :, None]) & live4[:, None, :], axis=2)
    codes = jnp.where(near[None] < 0, 2, listed.astype(jnp.int32)).reshape(-1)
    ahead = q0 + jnp.arange(2, dtype=jnp.int32) - 3
    cvis = live4[:, None, :] & (column_blocks[:, None, :] <= ahead[None, :, None])
    cbias = jnp.where(cvis, 0.0, NEG).astype(jnp.float32)
    cbias = jnp.broadcast_to(cbias.reshape(HEADS * 2, VSLOTS, 1), (HEADS * 2, VSLOTS, BLOCK))
    cbias = cbias.reshape(HEADS * 2, VSLOTS * BLOCK)

    def run(Q, R, collective_id):
        mine = first & (device == c * 2 + k)
        turn = jnp.arange(R * 8, dtype=jnp.int32)
        hit = mine[None] & (rank[None] % (8 * R) == turn[:, None])
        sel = jnp.sum(jnp.where(hit, group * 2 + block % 2, 0), axis=1, dtype=jnp.int32)
        wanted = jnp.arange(Q, dtype=jnp.int32) * 8 + c // 8
        hit = (first & (core == k))[None] & (rank[None] == wanted[:, None])
        own = jnp.sum(jnp.where(hit, block // 4, 0), axis=1, dtype=jnp.int32)
        slots = jnp.where(live, core * (Q * 8) + rank, 0)
        pairs, halo = gather_pairs(sel, own, kv.reshape(16, BLOCK, 256), Q, R, collective_id)
        return attend(
            slots, codes, queries, kv, halo.reshape(KV_HEADS, 256, 256), base, cbias,
            pairs.reshape(2 * Q * 8, BLOCK, 256),
        )

    small = (most <= 7 * 8) & (load <= 8)
    return lax.cond(small, lambda: run(7, 1, 0), lambda: run(16, 2, 1))


def solution(mesh):
    placed = (
        P(("ctx", "head"), None, None),
        P(("ctx", "head"), None, None),
        P(("ctx", "head"), None, None),
        P(),
        P(),
        P(),
        P(),
    )
    return jax.shard_map(
        body, mesh=mesh, in_specs=placed, out_specs=P(("ctx", "head"), None, None), check_vma=False
    )
```

```python
import functools
import math

import jax
import jax.numpy as jnp
from jax import lax
from jax.experimental import pallas as pl
from jax.experimental.pallas import tpu as pltpu
from jax.sharding import PartitionSpec as P

HEADS = 32
KV_HEADS = 8
HDIM = 128
BLOCK = 128
VSLOTS = 4
SSLOTS = 16
BAND = 256
CTX = 64
SIDE = 4
NEG = -1e30
MESH = pl.DeviceIdType.MESH
BF16 = jnp.bfloat16
F32 = jnp.float32
FACTOR = 1.4426950408889634 / math.sqrt(HDIM)
NT = (((1,), (1,)), ((), ()))
SLOT, CODE, CSEE, SEL, OWN = 0, 128, 256, 512, 528
WORDS = 544


def kernel(
    Q, R, tab, base_ref, q_hbm, k_hbm, v_hbm, pk_hbm, pv_hbm, o_hbm,
    qv, kin, vin, pkin, pvin, kvt, halo, send, recv, home, g_all, tables, qt, acc, tops, outs,
    in_sem, out_sem, s1_send, s1_recv, a_send, a_recv, b_send, b_recv, sib_send, sib_recv,
):
    c = lax.axis_index("ctx")
    k = lax.axis_index("head")
    coords = (c // 16, (c // 4) % 4, c % 4)
    fetch = [
        pltpu.make_async_copy(k_hbm, kin, in_sem.at[0]),
        pltpu.make_async_copy(v_hbm, vin, in_sem.at[1]),
        pltpu.make_async_copy(q_hbm, qv, in_sem.at[2]),
        pltpu.make_async_copy(pk_hbm, pkin, in_sem.at[3]),
        pltpu.make_async_copy(pv_hbm, pvin, in_sem.at[4]),
    ]
    for copy in fetch:
        copy.start()
    barrier = pltpu.get_barrier_semaphore()

    @pl.loop(1, CTX)
    def _(d):
        pl.semaphore_signal(barrier, inc=1, device_id={"ctx": (c + d) % CTX}, device_id_type=MESH)

    pl.semaphore_signal(barrier, inc=1, device_id={"head": 1 - k}, device_id_type=MESH)

    fetch[0].wait()
    fetch[1].wait()
    kt = jnp.swapaxes(kin[...], 0, 1)
    vt = jnp.swapaxes(vin[...], 0, 1)
    kvt[:, :, :HDIM] = kt.reshape(16, BLOCK, HDIM)
    kvt[:, :, HDIM:] = vt.reshape(16, BLOCK, HDIM)
    for r in range(R):
        for u in range(8):
            send[r, u] = kvt[tab[SEL + r * 8 + u]]
    pl.semaphore_wait(barrier, CTX)

    @pl.loop(1, CTX)
    def _(d):
        p = (c + d) % CTX
        for r in range(R):
            pltpu.make_async_remote_copy(
                src_ref=send.at[r, p // 8, pl.ds((p % 8) * 16, 16)],
                dst_ref=recv.at[r, c],
                send_sem=s1_send,
                recv_sem=s1_recv,
                device_id={"ctx": p},
                device_id_type=MESH,
            ).start()

    for r in range(R):
        recv[r, c] = send[r, c // 8, pl.ds((c % 8) * 16, 16)]

    fetch[3].wait()
    fetch[4].wait()
    halo[:, :, :HDIM] = jnp.swapaxes(pkin[...], 0, 1).reshape(16, BLOCK, HDIM)
    halo[:, :, HDIM:] = jnp.swapaxes(pvin[...], 0, 1).reshape(16, BLOCK, HDIM)

    fetch[2].wait()

    for i in range(2):
        qt[i * 16 : i * 16 + 16] = jnp.swapaxes(qv[:, i * 16 : i * 16 + 16, :], 0, 1)

    @pl.loop(0, HEADS)
    def _(h):
        line = jnp.broadcast_to(base_ref[pl.ds(h, 1), :], (BLOCK, 3 * BLOCK))
        tables[h] = pltpu.roll(line, 0, 1, stride=1, stride_axis=0)

    row = lax.broadcasted_iota(jnp.int32, (BLOCK, BLOCK), 0)
    col = lax.broadcasted_iota(jnp.int32, (BLOCK, BLOCK), 1)
    triangle = jnp.where(col <= row, 0.0, NEG)
    ones = jnp.ones((3 * BLOCK, HDIM), BF16)

    def band(first, last):
        @pl.loop(first, last)
        def _(g):
            blocks = [halo[2 * g], halo[2 * g + 1], kvt[2 * g], kvt[2 * g + 1]]
            for j in range(2):
                window = jnp.concatenate(blocks[j : j + 3], axis=0)
                rows = qt[pl.ds(g * 4, 4), j * BLOCK : (j + 1) * BLOCK, :]
                score = lax.dot_general(
                    rows.reshape(4 * BLOCK, HDIM), window[:, :HDIM], NT, preferred_element_type=F32
                )
                weights = []
                for hh in range(4):
                    h = g * 4 + hh
                    pieces = []
                    for w in range(3):
                        code = tab[CODE + h * 4 + j + w]
                        cut = slice(w * BLOCK, (w + 1) * BLOCK)
                        plain = tables[h, :, cut]
                        if w == 2:
                            bias = jnp.where(code == 1, triangle, plain)
                        else:
                            least = jnp.where(code == 1, 0.0, NEG)
                            most = jnp.where(code == 2, NEG, 0.0)
                            bias = jnp.minimum(jnp.maximum(plain, least), most)
                        pieces.append(score[hh * BLOCK : (hh + 1) * BLOCK, cut] + bias)
                    masked = jnp.concatenate(pieces, axis=1)
                    top = jnp.max(masked, axis=1, keepdims=True)
                    weights.append(jnp.exp2((masked - top) * FACTOR).astype(BF16))
                    tops[h, pl.ds(j * BLOCK, BLOCK), :] = jnp.broadcast_to(top, (BLOCK, HDIM))
                both = jnp.concatenate([window[:, HDIM:], ones], axis=1)
                mixed = jnp.dot(
                    jnp.concatenate(weights, axis=0), both, preferred_element_type=F32
                )
                acc[pl.ds(g * 4, 4), j * BLOCK : (j + 1) * BLOCK, :] = mixed.reshape(
                    4, BLOCK, 2 * HDIM
                )

    others = recv.at[:, pl.ds(0, CTX - 1)]
    pltpu.make_async_copy(others, others, s1_recv).wait()
    for q in range(Q):
        home[q] = recv[q % R, tab[OWN + q]]

    bounds = [0, (Q + 2) // 3, (2 * Q + 2) // 3, Q]

    def view(t, index, half=None):
        low, high = bounds[t], bounds[t + 1]
        middle = (low + high + 1) // 2
        if half == 0:
            high = middle
        if half == 1:
            low = middle
        x, y, z = index
        yh, yl = (slice(None), slice(None)) if y is None else (y // 2, y % 2)
        x = slice(None) if x is None else x
        z = slice(None) if z is None else z
        return g_all.at[pl.ds(k * Q + low, high - low), x, yh, yl, z]

    def moved(axis, delta, axis2=0, delta2=0):
        there = list(coords)
        there[axis] = (there[axis] + delta) % SIDE
        there[axis2] = (there[axis2] + delta2) % SIDE
        return {"ctx": there[0] * 16 + there[1] * 4 + there[2]}

    for t in range(3):
        low, high = bounds[t], bounds[t + 1]
        pltpu.make_async_copy(home.at[low:high], view(t, coords), a_recv.at[t]).start()

    @pl.loop(1, 16)
    def _(d):
        for t in range(3):
            low, high = bounds[t], bounds[t + 1]
            pltpu.make_async_remote_copy(
                src_ref=home.at[low:high], dst_ref=view(t, coords),
                send_sem=a_send.at[t], recv_sem=a_recv.at[t],
                device_id=moved(t, d // 4, (t + 1) % 3, d % 4), device_id_type=MESH,
            ).start()

    band(0, 4)

    across = []

    def to_sibling(ref):
        i = len(across)
        copy = pltpu.make_async_remote_copy(
            src_ref=ref, dst_ref=ref, send_sem=sib_send.at[i], recv_sem=sib_recv.at[i],
            device_id={"head": 1 - k}, device_id_type=MESH,
        )
        copy.start()
        across.append(copy)

    def slab(t, pos, half=None):
        index = [None, None, None]
        index[(t + 2) % 3] = pos
        return view(t, index, half)

    def push(t, pos, half, i, delta):
        ref = slab(t, pos, half)
        copy = pltpu.make_async_remote_copy(
            src_ref=ref, dst_ref=ref, send_sem=b_send.at[t, i], recv_sem=b_recv.at[t, i],
            device_id=moved((t + 2) % 3, delta), device_id_type=MESH,
        )
        copy.start()
        return copy

    sent = []
    for t in range(3):
        me = coords[(t + 2) % 3]
        whole = slab(t, me)
        pltpu.make_async_copy(whole, whole, a_recv.at[t]).wait()
        sent.append(
            [
                push(t, me, 0, 0, 1),
                push(t, me, 1, 1, -1),
                push(t, me, 1, 2, 1),
                push(t, me, 0, 3, -1),
            ]
        )
    for t in range(3):
        to_sibling(slab(t, coords[(t + 2) % 3]))
    band(4, 6)
    for t in range(3):
        me = coords[(t + 2) % 3]
        left, right = (me + 3) % 4, (me + 1) % 4
        sent[t][0].wait_recv()
        sent[t].append(push(t, left, 0, 4, 1))
        sent[t][1].wait_recv()
        sent[t].append(push(t, right, 1, 5, -1))
        to_sibling(slab(t, left, 0))
        to_sibling(slab(t, right, 1))
    band(6, 8)
    for t in range(3):
        me = coords[(t + 2) % 3]
        left, right = (me + 3) % 4, (me + 1) % 4
        sent[t][2].wait_recv()
        to_sibling(slab(t, left, 1))
        sent[t][3].wait_recv()
        to_sibling(slab(t, right, 0))
    for t in range(3):
        opposite = (coords[(t + 2) % 3] + 2) % 4
        sent[t][4].wait_recv()
        to_sibling(slab(t, opposite, 0))
        sent[t][5].wait_recv()
        to_sibling(slab(t, opposite, 1))
    for copy in across:
        copy.wait_recv()

    ones4 = jnp.ones((VSLOTS * BLOCK, HDIM), BF16)

    def columns_of(first, last):
        @pl.loop(first, last, step=4)
        def _(base):
            heads = [base + i for i in range(4)]
            loaded, scores = [], []
            for h in heads:
                tiles = []
                for s in range(VSLOTS):
                    at = tab[SLOT + h * VSLOTS + s]
                    tile = g_all[at // 8, (at % 8) // 2, at % 2]
                    tiles.append(tile.reshape(BLOCK, 2 * HDIM))
                columns = jnp.concatenate(tiles, axis=0)
                loaded.append(columns)
                scores.append(
                    lax.dot_general(qt[h], columns[:, :HDIM], NT, preferred_element_type=F32)
                )
            ready = []
            for h, score in zip(heads, scores):
                parts = []
                for j in range(2):
                    pieces = []
                    for s in range(VSLOTS):
                        see = tab[CSEE + (h * 2 + j) * VSLOTS + s]
                        bias = jnp.where(see == 1, 0.0, NEG)
                        pieces.append(
                            score[j * BLOCK : (j + 1) * BLOCK, s * BLOCK : (s + 1) * BLOCK] + bias
                        )
                    parts.append(jnp.concatenate(pieces, axis=1))
                masked = jnp.concatenate(parts, axis=0)
                top = tops[h]
                new = jnp.maximum(top, jnp.max(masked, axis=1, keepdims=True))
                weights = jnp.exp2((masked - new[:, :1]) * FACTOR).astype(BF16)
                ready.append((weights, jnp.exp2((top - new) * FACTOR)))
            for h, columns, (weights, keep) in zip(heads, loaded, ready):
                both = jnp.concatenate([columns[:, HDIM:], ones4], axis=1)
                mixed = jnp.dot(weights, both, preferred_element_type=F32)
                upper = acc[h, :, :HDIM] * keep + mixed[:, :HDIM]
                lower = acc[h, :, HDIM:] * keep + mixed[:, HDIM:]
                qt[h] = (upper / lower).astype(BF16)

    for i in range(2):
        sixteen = slice(i * 16, i * 16 + 16)
        columns_of(i * 16, i * 16 + 16)
        outs[i] = jnp.swapaxes(qt[sixteen], 0, 1)
        pltpu.make_async_copy(outs.at[i], o_hbm.at[:, sixteen, :], out_sem.at[i]).start()
    for i in range(2):
        sixteen = slice(i * 16, i * 16 + 16)
        pltpu.make_async_copy(outs.at[i], o_hbm.at[:, sixteen, :], out_sem.at[i]).wait()
    for t in range(3):
        for copy in sent[t]:
            copy.wait_send()
    for copy in across:
        copy.wait_send()
    for t in range(3):
        low, high = bounds[t], bounds[t + 1]
        for d in range(15):
            pltpu.make_async_copy(home.at[low:high], home.at[low:high], a_send.at[t]).wait()
    pltpu.make_async_copy(others, others, s1_send).wait()


def attend(table, base, queries, keys, values, before_keys, before_values, Q, R, collective_id):
    dma = pltpu.SemaphoreType.DMA
    return pl.pallas_call(
        functools.partial(kernel, Q, R),
        out_shape=jax.ShapeDtypeStruct(queries.shape, BF16),
        in_specs=[
            pl.BlockSpec(memory_space=pltpu.SMEM),
            pl.BlockSpec(memory_space=pltpu.VMEM),
            pl.BlockSpec(memory_space=pl.ANY),
            pl.BlockSpec(memory_space=pl.ANY),
            pl.BlockSpec(memory_space=pl.ANY),
            pl.BlockSpec(memory_space=pl.ANY),
            pl.BlockSpec(memory_space=pl.ANY),
        ],
        out_specs=pl.BlockSpec(memory_space=pl.ANY),
        scratch_shapes=[
            pltpu.VMEM((256, HEADS, HDIM), BF16),
            pltpu.VMEM((256, KV_HEADS, HDIM), BF16),
            pltpu.VMEM((256, KV_HEADS, HDIM), BF16),
            pltpu.VMEM((256, KV_HEADS, HDIM), BF16),
            pltpu.VMEM((256, KV_HEADS, HDIM), BF16),
            pltpu.VMEM((16, BLOCK, 2 * HDIM), BF16),
            pltpu.VMEM((16, BLOCK, 2 * HDIM), BF16),
            pltpu.VMEM((R, 8, BLOCK, 2 * HDIM), BF16),
            pltpu.VMEM((R, CTX, 16, 2 * HDIM), BF16),
            pltpu.VMEM((Q, 16, 2 * HDIM), BF16),
            pltpu.VMEM((2 * Q, 4, 2, 2, 4, 16, 2 * HDIM), BF16),
            pltpu.VMEM((HEADS, BLOCK, 3 * BLOCK), F32),
            pltpu.VMEM((HEADS, 256, HDIM), BF16),
            pltpu.VMEM((HEADS, 256, 2 * HDIM), F32),
            pltpu.VMEM((HEADS, 256, HDIM), F32),
            pltpu.VMEM((2, 256, 16, HDIM), BF16),
            dma((5,)),
            dma((2,)),
            dma(()),
            dma(()),
            dma((3,)),
            dma((3,)),
            dma((3, 6)),
            dma((3, 6)),
            dma((21,)),
            dma((21,)),
        ],
        compiler_params=pltpu.CompilerParams(
            collective_id=collective_id, has_side_effects=True, vmem_limit_bytes=60 * 2**20
        ),
    )(table, base, queries, keys, values, before_keys, before_values)


def body(queries, key_states, value_states, column_blocks, column_count, slash_offsets, slash_count):
    c = lax.axis_index("ctx")
    k = lax.axis_index("head")

    route = [(i, i + 1) for i in range(2 * CTX - 1)]
    before_keys = lax.ppermute(key_states, ("ctx", "head"), route)
    before_values = lax.ppermute(value_states, ("ctx", "head"), route)

    block = column_blocks.reshape(HEADS * VSLOTS)
    index = jnp.arange(HEADS * VSLOTS, dtype=jnp.int32)
    live = (jnp.arange(VSLOTS, dtype=jnp.int32)[None] < column_count[:, None]).reshape(-1)
    group = index // (4 * VSLOTS)
    pid = block * KV_HEADS + group
    core = (block // 2) % 2
    device = block // 2
    first = live & ~jnp.any(
        (pid[:, None] == pid[None]) & live[None] & (index[None] < index[:, None]), axis=1
    )
    same_core = first[None] & (core[None] == core[:, None])
    rank = jnp.sum(same_core & (pid[None] < pid[:, None]), axis=1, dtype=jnp.int32)
    load = jnp.sum(first[None] & (device[None] == device[:, None]), axis=1, dtype=jnp.int32)
    fits = jnp.all(~live | ((rank < 6 * 8) & (load <= 8)))

    olive = jnp.arange(SSLOTS, dtype=jnp.int32)[None] < slash_count[:, None]
    spot = jnp.arange(3 * BLOCK, dtype=jnp.int32)
    seen = jnp.any(
        (2 * BLOCK - spot[None, :, None] == slash_offsets[:, None, :]) & olive[:, None, :], axis=2
    )
    base = jnp.where(seen, 0.0, NEG).astype(F32)
    q0 = (c * 2 + k) * 2
    near = q0 - 2 + jnp.arange(4, dtype=jnp.int32)
    live4 = live.reshape(HEADS, VSLOTS)
    listed = jnp.any((column_blocks[:, None, :] == near[None, :, None]) & live4[:, None, :], axis=2)
    codes = jnp.where(near[None] < 0, 2, listed.astype(jnp.int32)).reshape(-1)
    ahead = q0 + jnp.arange(2, dtype=jnp.int32) - 3
    csee = live4[:, None, :] & (column_blocks[:, None, :] <= ahead[None, :, None])
    csee = csee.astype(jnp.int32).reshape(-1)

    def run(Q, R, collective_id):
        mine = first & (device == c * 2 + k)
        turn = jnp.arange(R * 8, dtype=jnp.int32)
        hit = mine[None] & (rank[None] % (8 * R) == turn[:, None])
        sel = jnp.sum(jnp.where(hit, group * 2 + block % 2, 0), axis=1, dtype=jnp.int32)
        wanted = jnp.arange(Q, dtype=jnp.int32) * 8 + c // 8
        hit = (first & (core == k))[None] & (rank[None] == wanted[:, None])
        own = jnp.sum(jnp.where(hit, block // 4, 0), axis=1, dtype=jnp.int32)
        slots = jnp.where(live, core * (Q * 8) + rank, 0)
        pad = lambda a: jnp.pad(a, (0, 16 - a.shape[0]))
        table = jnp.concatenate([slots, codes, csee, pad(sel), pad(own)])
        return attend(table, base, queries, key_states, value_states, before_keys, before_values, Q, R, collective_id)

    return lax.cond(fits, lambda: run(6, 1, 0), lambda: run(16, 2, 1))


def solution(mesh):
    placed = (
        P(("ctx", "head"), None, None),
        P(("ctx", "head"), None, None),
        P(("ctx", "head"), None, None),
        P(),
        P(),
        P(),
        P(),
    )
    return jax.shard_map(
        body, mesh=mesh, in_specs=placed, out_specs=P(("ctx", "head"), None, None), check_vma=False
    )
```

```python
import functools
import math

import jax
import jax.numpy as jnp
from jax import lax
from jax.experimental import pallas as pl
from jax.experimental.pallas import tpu as pltpu
from jax.sharding import PartitionSpec as P

HEADS = 32
KV_HEADS = 8
HDIM = 128
BLOCK = 128
VSLOTS = 4
SSLOTS = 16
BAND = 256
CTX = 64
SIDE = 4
NEG = -1e30
MESH = pl.DeviceIdType.MESH
BF16 = jnp.bfloat16
F32 = jnp.float32
FACTOR = 1.4426950408889634 / math.sqrt(HDIM)
NT = (((1,), (1,)), ((), ()))
SLOT, CODE, CSEE, REST, FITS = 0, 2, 3, 5, 6
SMALL = 6


def kernel(
    Q, R, t_hbm, off_hbm, cnt_hbm, q_hbm, k_hbm, v_hbm, o_hbm,
    tab, offsets, counts, qv, kin, vin, kvt, halo, send, recv, home, g_all, tables, qt, acc, tops, outs,
    in_sem, out_sem, s1_send, s1_recv, a_send, a_recv, b_send, b_recv, sib_send, sib_recv,
    halo_send, halo_recv,
):
    c = lax.axis_index("ctx")
    k = lax.axis_index("head")
    coords = (c // 16, (c // 4) % 4, c % 4)
    fetch = [
        pltpu.make_async_copy(k_hbm, kin, in_sem.at[0]),
        pltpu.make_async_copy(v_hbm, vin, in_sem.at[1]),
        pltpu.make_async_copy(q_hbm, qv, in_sem.at[2]),
        pltpu.make_async_copy(t_hbm, tab, in_sem.at[3]),
        pltpu.make_async_copy(off_hbm, offsets, in_sem.at[4]),
        pltpu.make_async_copy(cnt_hbm, counts, in_sem.at[5]),
    ]
    for copy in fetch:
        copy.start()
    barrier = pltpu.get_barrier_semaphore()

    @pl.loop(1, CTX)
    def _(d):
        pl.semaphore_signal(barrier, inc=1, device_id={"ctx": (c + d) % CTX}, device_id_type=MESH)

    pl.semaphore_signal(barrier, inc=1, device_id={"head": 1 - k}, device_id_type=MESH)

    @pl.when(k == 0)
    def _():
        pl.semaphore_signal(
            barrier, inc=1, device_id={"ctx": (c + CTX - 1) % CTX, "head": 1}, device_id_type=MESH
        )

    fetch[0].wait()
    fetch[1].wait()
    kt = jnp.swapaxes(kin[...], 0, 1)
    vt = jnp.swapaxes(vin[...], 0, 1)
    kvt[:, :, :HDIM] = kt.reshape(16, BLOCK, HDIM)
    kvt[:, :, HDIM:] = vt.reshape(16, BLOCK, HDIM)
    fetch[3].wait()
    for r in range(R):
        for u in range(8):
            send[r, u] = kvt[tab[REST, (0 if R == 1 else 16) + r * 8 + u]]
    pl.semaphore_wait(barrier, CTX + k)

    @pl.loop(1, CTX)
    def _(d):
        p = (c + d) % CTX
        for r in range(R):
            pltpu.make_async_remote_copy(
                src_ref=send.at[r, p // 8, pl.ds((p % 8) * 16, 16)],
                dst_ref=recv.at[r, c],
                send_sem=s1_send,
                recv_sem=s1_recv,
                device_id={"ctx": p},
                device_id_type=MESH,
            ).start()

    tails = []

    def pass_on(first, last):
        for g in range(first, last):
            copy = pltpu.make_async_remote_copy(
                src_ref=kvt.at[2 * g : 2 * g + 2], dst_ref=halo.at[2 * g : 2 * g + 2],
                send_sem=halo_send.at[g], recv_sem=halo_recv.at[g],
                device_id={"ctx": (c + k) % CTX, "head": 1 - k}, device_id_type=MESH,
            )
            copy.start()
            tails.append(copy)

    pass_on(0, 3)
    for r in range(R):
        recv[r, c] = send[r, c // 8, pl.ds((c % 8) * 16, 16)]

    fetch[2].wait()

    for i in range(2):
        qt[i * 16 : i * 16 + 16] = jnp.swapaxes(qv[:, i * 16 : i * 16 + 16, :], 0, 1)

    fetch[4].wait()
    fetch[5].wait()
    spot = 2 * BLOCK - lax.broadcasted_iota(jnp.int32, (1, 3 * BLOCK), 1)

    @pl.loop(0, HEADS)
    def _(h):
        used = counts[h]
        line = jnp.full((1, 3 * BLOCK), NEG, F32)
        for s in range(SSLOTS):
            offset = jnp.where(s < used, offsets[s, h], -1000)
            line = jnp.where(spot == offset, 0.0, line)
        line = jnp.broadcast_to(line, (BLOCK, 3 * BLOCK))
        tables[h] = pltpu.roll(line, 0, 1, stride=1, stride_axis=0)

    row = lax.broadcasted_iota(jnp.int32, (BLOCK, BLOCK), 0)
    col = lax.broadcasted_iota(jnp.int32, (BLOCK, BLOCK), 1)
    triangle = jnp.where(col <= row, 0.0, NEG)
    ones = jnp.ones((3 * BLOCK, HDIM), BF16)

    def band(first, last):
        for g in range(first, last):
            tails[g].wait_recv()

        @pl.loop(first, last)
        def _(g):
            blocks = [halo[2 * g], halo[2 * g + 1], kvt[2 * g], kvt[2 * g + 1]]
            for j in range(2):
                window = jnp.concatenate(blocks[j : j + 3], axis=0)
                rows = qt[pl.ds(g * 4, 4), j * BLOCK : (j + 1) * BLOCK, :]
                score = lax.dot_general(
                    rows.reshape(4 * BLOCK, HDIM), window[:, :HDIM], NT, preferred_element_type=F32
                )
                weights = []
                for hh in range(4):
                    h = g * 4 + hh
                    pieces = []
                    for w in range(3):
                        code = tab[CODE, h * 4 + j + w]
                        cut = slice(w * BLOCK, (w + 1) * BLOCK)
                        plain = tables[h, :, cut]
                        if w == 2:
                            bias = jnp.where(code == 1, triangle, plain)
                        else:
                            least = jnp.where(code == 1, 0.0, NEG)
                            most = jnp.where(code == 2, NEG, 0.0)
                            bias = jnp.minimum(jnp.maximum(plain, least), most)
                        pieces.append(score[hh * BLOCK : (hh + 1) * BLOCK, cut] + bias)
                    masked = jnp.concatenate(pieces, axis=1)
                    top = jnp.max(masked, axis=1, keepdims=True)
                    weights.append(jnp.exp2((masked - top) * FACTOR).astype(BF16))
                    tops[h, pl.ds(j * BLOCK, BLOCK), :] = jnp.broadcast_to(top, (BLOCK, HDIM))
                both = jnp.concatenate([window[:, HDIM:], ones], axis=1)
                mixed = jnp.dot(
                    jnp.concatenate(weights, axis=0), both, preferred_element_type=F32
                )
                acc[pl.ds(g * 4, 4), j * BLOCK : (j + 1) * BLOCK, :] = mixed.reshape(
                    4, BLOCK, 2 * HDIM
                )

    others = recv.at[:, pl.ds(0, CTX - 1)]
    pltpu.make_async_copy(others, others, s1_recv).wait()
    for q in range(Q):
        home[q] = recv[q % R, tab[REST, (32 if R == 1 else 48) + q]]

    bounds = [0, (Q + 2) // 3, (2 * Q + 2) // 3, Q]

    def view(t, index, half=None):
        low, high = bounds[t], bounds[t + 1]
        middle = (low + high + 1) // 2
        if half == 0:
            high = middle
        if half == 1:
            low = middle
        x, y, z = index
        yh, yl = (slice(None), slice(None)) if y is None else (y // 2, y % 2)
        x = slice(None) if x is None else x
        z = slice(None) if z is None else z
        return g_all.at[pl.ds(k * Q + low, high - low), x, yh, yl, z]

    def moved(axis, delta, axis2=0, delta2=0):
        there = list(coords)
        there[axis] = (there[axis] + delta) % SIDE
        there[axis2] = (there[axis2] + delta2) % SIDE
        return {"ctx": there[0] * 16 + there[1] * 4 + there[2]}

    for t in range(3):
        low, high = bounds[t], bounds[t + 1]
        pltpu.make_async_copy(home.at[low:high], view(t, coords), a_recv.at[t]).start()

    for t in range(3):
        low, high = bounds[t], bounds[t + 1]

        @pl.loop(1, 16)
        def _(d):
            pltpu.make_async_remote_copy(
                src_ref=home.at[low:high], dst_ref=view(t, coords),
                send_sem=a_send.at[t], recv_sem=a_recv.at[t],
                device_id=moved(t, d // 4, (t + 1) % 3, d % 4), device_id_type=MESH,
            ).start()

    pass_on(3, 7)
    band(0, 2)

    across = []

    def to_sibling(ref):
        i = len(across)
        copy = pltpu.make_async_remote_copy(
            src_ref=ref, dst_ref=ref, send_sem=sib_send.at[i], recv_sem=sib_recv.at[i],
            device_id={"head": 1 - k}, device_id_type=MESH,
        )
        copy.start()
        across.append(copy)

    def slab(t, pos, half=None):
        index = [None, None, None]
        index[(t + 2) % 3] = pos
        return view(t, index, half)

    def push(t, pos, half, i, delta):
        ref = slab(t, pos, half)
        copy = pltpu.make_async_remote_copy(
            src_ref=ref, dst_ref=ref, send_sem=b_send.at[t, i], recv_sem=b_recv.at[t, i],
            device_id=moved((t + 2) % 3, delta), device_id_type=MESH,
        )
        copy.start()
        return copy

    sent = []
    for t in range(3):
        me = coords[(t + 2) % 3]
        whole = slab(t, me)
        pltpu.make_async_copy(whole, whole, a_recv.at[t]).wait()
        sent.append(
            [
                push(t, me, 0, 0, 1),
                push(t, me, 1, 1, -1),
                push(t, me, 1, 2, 1),
                push(t, me, 0, 3, -1),
            ]
        )
    for t in range(3):
        to_sibling(slab(t, coords[(t + 2) % 3]))
    pass_on(7, 8)
    band(2, 3)
    for t in range(3):
        me = coords[(t + 2) % 3]
        left, right = (me + 3) % 4, (me + 1) % 4
        sent[t][0].wait_recv()
        sent[t].append(push(t, left, 0, 4, 1))
        sent[t][1].wait_recv()
        sent[t].append(push(t, right, 1, 5, -1))
        to_sibling(slab(t, left, 0))
        to_sibling(slab(t, right, 1))
    band(3, 6)
    for t in range(3):
        me = coords[(t + 2) % 3]
        left, right = (me + 3) % 4, (me + 1) % 4
        sent[t][2].wait_recv()
        to_sibling(slab(t, left, 1))
        sent[t][3].wait_recv()
        to_sibling(slab(t, right, 0))
    for t in range(3):
        opposite = (coords[(t + 2) % 3] + 2) % 4
        sent[t][4].wait_recv()
        to_sibling(slab(t, opposite, 0))
        sent[t][5].wait_recv()
        to_sibling(slab(t, opposite, 1))
    band(6, 8)
    for copy in across:
        copy.wait_recv()

    ones4 = jnp.ones((VSLOTS * BLOCK, HDIM), BF16)

    def columns_of(first, last):
        @pl.loop(first, last, step=8)
        def _(base):
            def scored(h):
                tiles = []
                for s in range(VSLOTS):
                    at = tab[SLOT + (R > 1), h * VSLOTS + s]
                    tile = g_all[at // 8, (at % 8) // 2, at % 2]
                    tiles.append(tile.reshape(BLOCK, 2 * HDIM))
                columns = jnp.concatenate(tiles, axis=0)
                score = lax.dot_general(qt[h], columns[:, :HDIM], NT, preferred_element_type=F32)
                return columns, score

            def weighted(h, score):
                parts = []
                for j in range(2):
                    pieces = []
                    for s in range(VSLOTS):
                        see = tab[CSEE + j, h * VSLOTS + s]
                        bias = jnp.where(see == 1, 0.0, NEG)
                        pieces.append(
                            score[j * BLOCK : (j + 1) * BLOCK, s * BLOCK : (s + 1) * BLOCK] + bias
                        )
                    parts.append(jnp.concatenate(pieces, axis=1))
                masked = jnp.concatenate(parts, axis=0)
                top = tops[h]
                new = jnp.maximum(top, jnp.max(masked, axis=1, keepdims=True))
                weights = jnp.exp2((masked - new[:, :1]) * FACTOR).astype(BF16)
                return weights, jnp.exp2((top - new) * FACTOR)

            def finished(h, columns, weights, keep):
                both = jnp.concatenate([columns[:, HDIM:], ones4], axis=1)
                mixed = jnp.dot(weights, both, preferred_element_type=F32)
                upper = acc[h, :, :HDIM] * keep + mixed[:, :HDIM]
                lower = acc[h, :, HDIM:] * keep + mixed[:, HDIM:]
                qt[h] = (upper / lower).astype(BF16)

            ahead = scored(base)
            for i in range(8):
                h = base + i
                columns, score = ahead
                if i < 7:
                    ahead = scored(h + 1)
                finished(h, columns, *weighted(h, score))

    for i in range(2):
        sixteen = slice(i * 16, i * 16 + 16)
        columns_of(i * 16, i * 16 + 16)
        outs[i] = jnp.swapaxes(qt[sixteen], 0, 1)
        pltpu.make_async_copy(outs.at[i], o_hbm.at[:, sixteen, :], out_sem.at[i]).start()
    for i in range(2):
        sixteen = slice(i * 16, i * 16 + 16)
        pltpu.make_async_copy(outs.at[i], o_hbm.at[:, sixteen, :], out_sem.at[i]).wait()
    for t in range(3):
        for copy in sent[t]:
            copy.wait_send()
    for copy in across:
        copy.wait_send()
    for t in range(3):
        low, high = bounds[t], bounds[t + 1]
        for d in range(15):
            pltpu.make_async_copy(home.at[low:high], home.at[low:high], a_send.at[t]).wait()
    for copy in tails:
        copy.wait_send()
    pltpu.make_async_copy(others, others, s1_send).wait()


def attend(table, offsets, counts, queries, keys, values, Q, R, collective_id):
    dma = pltpu.SemaphoreType.DMA
    return pl.pallas_call(
        functools.partial(kernel, Q, R),
        out_shape=jax.ShapeDtypeStruct(queries.shape, BF16),
        in_specs=[
            pl.BlockSpec(memory_space=pl.ANY),
            pl.BlockSpec(memory_space=pl.ANY),
            pl.BlockSpec(memory_space=pl.ANY),
            pl.BlockSpec(memory_space=pl.ANY),
            pl.BlockSpec(memory_space=pl.ANY),
            pl.BlockSpec(memory_space=pl.ANY),
        ],
        out_specs=pl.BlockSpec(memory_space=pl.ANY),
        scratch_shapes=[
            pltpu.SMEM((8, 128), jnp.int32),
            pltpu.SMEM((SSLOTS, HEADS), jnp.int32),
            pltpu.SMEM((HEADS,), jnp.int32),
            pltpu.VMEM((256, HEADS, HDIM), BF16),
            pltpu.VMEM((256, KV_HEADS, HDIM), BF16),
            pltpu.VMEM((256, KV_HEADS, HDIM), BF16),
            pltpu.VMEM((16, BLOCK, 2 * HDIM), BF16),
            pltpu.VMEM((16, BLOCK, 2 * HDIM), BF16),
            pltpu.VMEM((R, 8, BLOCK, 2 * HDIM), BF16),
            pltpu.VMEM((R, CTX, 16, 2 * HDIM), BF16),
            pltpu.VMEM((Q, 16, 2 * HDIM), BF16),
            pltpu.VMEM((2 * Q, 4, 2, 2, 4, 16, 2 * HDIM), BF16),
            pltpu.VMEM((HEADS, BLOCK, 3 * BLOCK), F32),
            pltpu.VMEM((HEADS, 256, HDIM), BF16),
            pltpu.VMEM((HEADS, 256, 2 * HDIM), F32),
            pltpu.VMEM((HEADS, 256, HDIM), F32),
            pltpu.VMEM((2, 256, 16, HDIM), BF16),
            dma((6,)),
            dma((2,)),
            dma(()),
            dma(()),
            dma((3,)),
            dma((3,)),
            dma((3, 6)),
            dma((3, 6)),
            dma((21,)),
            dma((21,)),
            dma((8,)),
            dma((8,)),
        ],
        compiler_params=pltpu.CompilerParams(
            collective_id=collective_id, has_side_effects=True, vmem_limit_bytes=60 * 2**20
        ),
    )(table, offsets, counts, queries, keys, values)


def table_kernel(blocks_hbm, counts_hbm, o_ref, blocks, counts, column, sems):
    copies = [
        pltpu.make_async_copy(blocks_hbm, blocks, sems.at[0]),
        pltpu.make_async_copy(counts_hbm, counts, sems.at[1]),
    ]
    for copy in copies:
        copy.start()
    c = lax.axis_index("ctx")
    k = lax.axis_index("head")
    for copy in copies:
        copy.wait()
    for i in range(HEADS * VSLOTS):
        block = blocks[i % VSLOTS, i // VSLOTS]
        block = jnp.where(i % VSLOTS < counts[i // VSLOTS], block, block + 1024)
        column[pl.ds(i, 1), :] = jnp.full((1, 128), block, jnp.int32)
    shape = (128, 128)
    down, across = column[...], column[...].astype(F32).T.astype(jnp.int32)
    i, j = lax.broadcasted_iota(jnp.int32, shape, 0), lax.broadcasted_iota(jnp.int32, shape, 1)
    live_i, live_j = down < 1024, across < 1024
    pid_i = down * KV_HEADS + i // 16
    pid_j = across * KV_HEADS + j // 16
    core_i, core_j = (down // 2) % 2, (across // 2) % 2
    same = pid_i == pid_j

    def total(mask, axis):
        return jnp.sum(jnp.where(mask, 1.0, 0.0), axis=axis, keepdims=True).astype(jnp.int32)

    def wide(a):
        return jnp.broadcast_to(a, shape)

    first_i = live_i & (wide(total(same & live_j & (j < i), 1)) == 0)
    first_j = live_j & (wide(total(same & live_i & (i < j), 0)) == 0)
    rank_i = wide(total(first_j & (core_i == core_j) & (pid_j < pid_i), 1))
    rank_j = wide(total(first_i & (core_i == core_j) & (pid_i < pid_j), 0))
    load_i = wide(total(first_j & (down // 2 == across // 2), 1))
    bad = total(live_i & ((rank_i >= SMALL * 8) | (load_i > 8)), 0)
    q0 = (c * 2 + k) * 2
    near = q0 - 2 + j % 4
    listed = total(live_i & (i // 4 == j // 4) & (down == near), 0)
    codes = jnp.where(near[:1] < 0, 2, jnp.minimum(listed, 1))
    mine = first_i & (down // 2 == c * 2 + k)
    kept = first_i & (core_i == k) & (rank_i == (j % 16) * 8 + c // 8)
    hit = jnp.where(
        j < 16,
        jnp.where(mine & (rank_i % 8 == j), 1, 0),
        jnp.where(
            j < 32, jnp.where(mine & (rank_i % 16 == j - 16), 1, 0), jnp.where(kept, 1, 0)
        ),
    )
    value = jnp.where(j < 32, (i // 16) * 2 + down % 2, down // 4)
    rest = jnp.sum(jnp.where(hit == 1, value, 0).astype(F32), axis=0, keepdims=True)

    def seen(ahead):
        return jnp.where(across[:1] <= ahead, 1, 0)

    for row, q in ((0, SMALL), (1, 16)):
        place = core_j[:1] * (q * 8) + rank_j[:1]
        o_ref[row : row + 1, :] = jnp.where(across[:1] < 1024, place, 0)
    o_ref[CODE : CODE + 1, :] = codes
    o_ref[CSEE : CSEE + 1, :] = seen(q0 - 3)
    o_ref[CSEE + 1 : CSEE + 2, :] = seen(q0 - 2)
    o_ref[REST : REST + 1, :] = rest.astype(jnp.int32)
    o_ref[FITS : FITS + 1, :] = jnp.where(bad == 0, 1, 0)
    o_ref[FITS + 1 : FITS + 2, :] = jnp.zeros((1, 128), jnp.int32)


def tables_of(column_blocks, column_count):
    return pl.pallas_call(
        table_kernel,
        out_shape=jax.ShapeDtypeStruct((8, 128), jnp.int32),
        in_specs=[pl.BlockSpec(memory_space=pl.ANY), pl.BlockSpec(memory_space=pl.ANY)],
        out_specs=pl.BlockSpec(memory_space=pltpu.VMEM),
        scratch_shapes=[
            pltpu.SMEM((VSLOTS, HEADS), jnp.int32),
            pltpu.SMEM((HEADS,), jnp.int32),
            pltpu.VMEM((128, 128), jnp.int32),
            pltpu.SemaphoreType.DMA((2,)),
        ],
        cost_estimate=pl.CostEstimate(flops=10**6, bytes_accessed=10**5, transcendentals=0),
    )(column_blocks, column_count)


def body(queries, key_states, value_states, column_blocks, column_count, slash_offsets, slash_count):
    table = tables_of(column_blocks.T, column_count)
    offsets = slash_offsets.T

    def run(Q, R, collective_id):
        return attend(
            table, offsets, slash_count, queries, key_states, value_states,
            Q, R, collective_id,
        )

    return lax.cond(table[FITS, 0] == 1, lambda: run(SMALL, 1, 0), lambda: run(16, 2, 1))


def solution(mesh):
    placed = (
        P(("ctx", "head"), None, None),
        P(("ctx", "head"), None, None),
        P(("ctx", "head"), None, None),
        P(),
        P(),
        P(),
        P(),
    )
    return jax.shard_map(
        body, mesh=mesh, in_specs=placed, out_specs=P(("ctx", "head"), None, None), check_vma=False
    )
```

```python
import functools
import math

import jax
import jax.numpy as jnp
from jax import lax
from jax.experimental import pallas as pl
from jax.experimental.pallas import tpu as pltpu
from jax.sharding import PartitionSpec as P

HEADS = 32
KV_HEADS = 8
HDIM = 128
BLOCK = 128
VSLOTS = 4
SSLOTS = 16
BAND = 256
CTX = 64
SIDE = 4
NEG = -1e30
MESH = pl.DeviceIdType.MESH
BF16 = jnp.bfloat16
F32 = jnp.float32
FACTOR = 1.4426950408889634 / math.sqrt(HDIM)
NT = (((1,), (1,)), ((), ()))
CODE, CSEE, REST, LEVEL = 3, 4, 6, 7
FORMS = ((12, 1), (14, 2), (32, 4))


def kernel(
    form, t_hbm, off_hbm, cnt_hbm, q_hbm, k_hbm, v_hbm, o_hbm,
    tab, offsets, counts, qv, kin, vin, kvt, halo, send, recv, home, g_all, tables, qt, acc, tops, outs,
    in_sem, out_sem, s1_send, s1_recv, a_send, a_recv, b_send, b_recv, sib_send, sib_recv,
    halo_send, halo_recv,
):
    Q, R = FORMS[form]
    c = lax.axis_index("ctx")
    k = lax.axis_index("head")
    coords = (c // 16, (c // 4) % 4, c % 4)
    fetch = [
        pltpu.make_async_copy(k_hbm, kin, in_sem.at[0]),
        pltpu.make_async_copy(v_hbm, vin, in_sem.at[1]),
        pltpu.make_async_copy(q_hbm, qv, in_sem.at[2]),
        pltpu.make_async_copy(t_hbm, tab, in_sem.at[3]),
        pltpu.make_async_copy(off_hbm, offsets, in_sem.at[4]),
        pltpu.make_async_copy(cnt_hbm, counts, in_sem.at[5]),
    ]
    for copy in fetch:
        copy.start()
    barrier = pltpu.get_barrier_semaphore()

    @pl.loop(1, CTX)
    def _(d):
        pl.semaphore_signal(barrier, inc=1, device_id={"ctx": (c + d) % CTX}, device_id_type=MESH)

    pl.semaphore_signal(barrier, inc=1, device_id={"head": 1 - k}, device_id_type=MESH)

    @pl.when(k == 0)
    def _():
        pl.semaphore_signal(
            barrier, inc=1, device_id={"ctx": (c + CTX - 1) % CTX, "head": 1}, device_id_type=MESH
        )

    fetch[0].wait()
    fetch[1].wait()
    kt = jnp.swapaxes(kin[...], 0, 1)
    vt = jnp.swapaxes(vin[...], 0, 1)
    kvt[:, :, :HDIM] = kt.reshape(16, BLOCK, HDIM)
    kvt[:, :, HDIM:] = vt.reshape(16, BLOCK, HDIM)
    fetch[3].wait()
    for r in range(R):
        for u in range(4):
            pair = kvt[tab[REST, (0, 8, 16)[form] + r * 4 + u]]
            send[r, u, 0] = pair[:, :HDIM]
            send[r, u, 1] = pair[:, HDIM:]
    pl.semaphore_wait(barrier, CTX + k)

    @pl.loop(1, CTX)
    def _(d):
        p = (c + d) % CTX
        for r in range(R):
            pltpu.make_async_remote_copy(
                src_ref=send.at[r, p // 16, (p // 8) % 2, pl.ds((p % 8) * 16, 16)],
                dst_ref=recv.at[r, c],
                send_sem=s1_send,
                recv_sem=s1_recv,
                device_id={"ctx": p},
                device_id_type=MESH,
            ).start()

    tails = []

    def pass_on(first, last):
        for g in range(first, last):
            copy = pltpu.make_async_remote_copy(
                src_ref=kvt.at[2 * g : 2 * g + 2], dst_ref=halo.at[2 * g : 2 * g + 2],
                send_sem=halo_send.at[g], recv_sem=halo_recv.at[g],
                device_id={"ctx": (c + k) % CTX, "head": 1 - k}, device_id_type=MESH,
            )
            copy.start()
            tails.append(copy)

    pass_on(0, 3)
    for r in range(R):
        recv[r, c] = send[r, c // 16, (c // 8) % 2, pl.ds((c % 8) * 16, 16)]

    fetch[2].wait()

    for i in range(2):
        qt[i * 16 : i * 16 + 16] = jnp.swapaxes(qv[:, i * 16 : i * 16 + 16, :], 0, 1)

    fetch[4].wait()
    fetch[5].wait()
    spot = 2 * BLOCK - lax.broadcasted_iota(jnp.int32, (1, 3 * BLOCK), 1)

    @pl.loop(0, HEADS)
    def _(h):
        used = counts[h]
        line = jnp.full((1, 3 * BLOCK), NEG, F32)
        for s in range(SSLOTS):
            offset = jnp.where(s < used, offsets[s, h], -1000)
            line = jnp.where(spot == offset, 0.0, line)
        line = jnp.broadcast_to(line, (BLOCK, 3 * BLOCK))
        tables[h] = pltpu.roll(line, 0, 1, stride=1, stride_axis=0)

    row = lax.broadcasted_iota(jnp.int32, (BLOCK, BLOCK), 0)
    col = lax.broadcasted_iota(jnp.int32, (BLOCK, BLOCK), 1)
    triangle = jnp.where(col <= row, 0.0, NEG)
    ones = jnp.ones((3 * BLOCK, HDIM), BF16)

    def band(first, last):
        for g in range(first, last):
            tails[g].wait_recv()

        @pl.loop(first, last)
        def _(g):
            blocks = [halo[2 * g], halo[2 * g + 1], kvt[2 * g], kvt[2 * g + 1]]
            for j in range(2):
                window = jnp.concatenate(blocks[j : j + 3], axis=0)
                rows = qt[pl.ds(g * 4, 4), j * BLOCK : (j + 1) * BLOCK, :]
                score = lax.dot_general(
                    rows.reshape(4 * BLOCK, HDIM), window[:, :HDIM], NT, preferred_element_type=F32
                )
                weights = []
                for hh in range(4):
                    h = g * 4 + hh
                    pieces = []
                    for w in range(3):
                        code = tab[CODE, h * 4 + j + w]
                        cut = slice(w * BLOCK, (w + 1) * BLOCK)
                        plain = tables[h, :, cut]
                        if w == 2:
                            bias = jnp.where(code == 1, triangle, plain)
                        else:
                            least = jnp.where(code == 1, 0.0, NEG)
                            most = jnp.where(code == 2, NEG, 0.0)
                            bias = jnp.minimum(jnp.maximum(plain, least), most)
                        pieces.append(score[hh * BLOCK : (hh + 1) * BLOCK, cut] + bias)
                    masked = jnp.concatenate(pieces, axis=1)
                    top = jnp.max(masked, axis=1, keepdims=True)
                    weights.append(jnp.exp2((masked - top) * FACTOR).astype(BF16))
                    tops[h, pl.ds(j * BLOCK, BLOCK), :] = jnp.broadcast_to(top, (BLOCK, HDIM))
                both = jnp.concatenate([window[:, HDIM:], ones], axis=1)
                mixed = jnp.dot(
                    jnp.concatenate(weights, axis=0), both, preferred_element_type=F32
                )
                acc[pl.ds(g * 4, 4), j * BLOCK : (j + 1) * BLOCK, :] = mixed.reshape(
                    4, BLOCK, 2 * HDIM
                )

    others = recv.at[:, pl.ds(0, CTX - 1)]
    pltpu.make_async_copy(others, others, s1_recv).wait()
    for q in range(Q):
        home[q] = recv[q % R, tab[REST, 32 + q]]

    bounds = [0, (Q + 2) // 3, (2 * Q + 2) // 3, Q]

    def view(t, index, half=None):
        low, high = bounds[t], bounds[t + 1]
        middle = (low + high + 1) // 2
        if half == 0:
            high = middle
        if half == 1:
            low = middle
        x, y, z = index
        yh, yl = (slice(None), slice(None)) if y is None else (y // 2, y % 2)
        x = slice(None) if x is None else x
        z = slice(None) if z is None else z
        return g_all.at[pl.ds(k * Q + low, high - low), x, yh, yl, z]

    def moved(axis, delta, axis2=0, delta2=0):
        there = list(coords)
        there[axis] = (there[axis] + delta) % SIDE
        there[axis2] = (there[axis2] + delta2) % SIDE
        return {"ctx": there[0] * 16 + there[1] * 4 + there[2]}

    for t in range(3):
        low, high = bounds[t], bounds[t + 1]
        pltpu.make_async_copy(home.at[low:high], view(t, coords), a_recv.at[t]).start()

    for t in range(3):
        low, high = bounds[t], bounds[t + 1]

        @pl.loop(1, 16)
        def _(d):
            pltpu.make_async_remote_copy(
                src_ref=home.at[low:high], dst_ref=view(t, coords),
                send_sem=a_send.at[t], recv_sem=a_recv.at[t],
                device_id=moved(t, d // 4, (t + 1) % 3, d % 4), device_id_type=MESH,
            ).start()

    pass_on(3, 7)
    band(0, 2)

    across = []

    def to_sibling(ref):
        i = len(across)
        copy = pltpu.make_async_remote_copy(
            src_ref=ref, dst_ref=ref, send_sem=sib_send.at[i], recv_sem=sib_recv.at[i],
            device_id={"head": 1 - k}, device_id_type=MESH,
        )
        copy.start()
        across.append(copy)

    def slab(t, pos, half=None):
        index = [None, None, None]
        index[(t + 2) % 3] = pos
        return view(t, index, half)

    def push(t, pos, half, i, delta):
        ref = slab(t, pos, half)
        copy = pltpu.make_async_remote_copy(
            src_ref=ref, dst_ref=ref, send_sem=b_send.at[t, i], recv_sem=b_recv.at[t, i],
            device_id=moved((t + 2) % 3, delta), device_id_type=MESH,
        )
        copy.start()
        return copy

    sent = []
    for t in range(3):
        me = coords[(t + 2) % 3]
        whole = slab(t, me)
        pltpu.make_async_copy(whole, whole, a_recv.at[t]).wait()
        sent.append(
            [
                push(t, me, 0, 0, 1),
                push(t, me, 1, 1, -1),
                push(t, me, 1, 2, 1),
                push(t, me, 0, 3, -1),
            ]
        )
    for t in range(3):
        to_sibling(slab(t, coords[(t + 2) % 3]))
    pass_on(7, 8)
    band(2, 3)
    for t in range(3):
        me = coords[(t + 2) % 3]
        left, right = (me + 3) % 4, (me + 1) % 4
        sent[t][0].wait_recv()
        sent[t].append(push(t, left, 0, 4, 1))
        sent[t][1].wait_recv()
        sent[t].append(push(t, right, 1, 5, -1))
        to_sibling(slab(t, left, 0))
        to_sibling(slab(t, right, 1))
    band(3, 6)
    for t in range(3):
        me = coords[(t + 2) % 3]
        left, right = (me + 3) % 4, (me + 1) % 4
        sent[t][2].wait_recv()
        to_sibling(slab(t, left, 1))
        sent[t][3].wait_recv()
        to_sibling(slab(t, right, 0))
    for t in range(3):
        opposite = (coords[(t + 2) % 3] + 2) % 4
        sent[t][4].wait_recv()
        to_sibling(slab(t, opposite, 0))
        sent[t][5].wait_recv()
        to_sibling(slab(t, opposite, 1))
    band(6, 8)
    for copy in across:
        copy.wait_recv()

    ones4 = jnp.ones((VSLOTS * BLOCK, HDIM), BF16)

    def columns_of(first, last):
        @pl.loop(first, last, step=8)
        def _(base):
            def scored(h):
                keys, values = [], []
                for s in range(VSLOTS):
                    at = tab[form, h * VSLOTS + s]
                    keys.append(g_all[at // 4, at % 4, 0].reshape(BLOCK, HDIM))
                    values.append(g_all[at // 4, at % 4, 1].reshape(BLOCK, HDIM))
                keys = jnp.concatenate(keys, axis=0)
                values = jnp.concatenate(values, axis=0)
                score = lax.dot_general(qt[h], keys, NT, preferred_element_type=F32)
                return values, score

            def weighted(h, score):
                parts = []
                for j in range(2):
                    pieces = []
                    for s in range(VSLOTS):
                        see = tab[CSEE + j, h * VSLOTS + s]
                        bias = jnp.where(see == 1, 0.0, NEG)
                        pieces.append(
                            score[j * BLOCK : (j + 1) * BLOCK, s * BLOCK : (s + 1) * BLOCK] + bias
                        )
                    parts.append(jnp.concatenate(pieces, axis=1))
                masked = jnp.concatenate(parts, axis=0)
                top = tops[h]
                new = jnp.maximum(top, jnp.max(masked, axis=1, keepdims=True))
                weights = jnp.exp2((masked - new[:, :1]) * FACTOR).astype(BF16)
                return weights, jnp.exp2((top - new) * FACTOR)

            def finished(h, values, weights, keep):
                both = jnp.concatenate([values, ones4], axis=1)
                mixed = jnp.dot(weights, both, preferred_element_type=F32)
                upper = acc[h, :, :HDIM] * keep + mixed[:, :HDIM]
                lower = acc[h, :, HDIM:] * keep + mixed[:, HDIM:]
                qt[h] = (upper / lower).astype(BF16)

            ahead = scored(base)
            for i in range(8):
                h = base + i
                values, score = ahead
                if i < 7:
                    ahead = scored(h + 1)
                finished(h, values, *weighted(h, score))

    for i in range(2):
        sixteen = slice(i * 16, i * 16 + 16)
        columns_of(i * 16, i * 16 + 16)
        outs[i] = jnp.swapaxes(qt[sixteen], 0, 1)
        pltpu.make_async_copy(outs.at[i], o_hbm.at[:, sixteen, :], out_sem.at[i]).start()
    for i in range(2):
        sixteen = slice(i * 16, i * 16 + 16)
        pltpu.make_async_copy(outs.at[i], o_hbm.at[:, sixteen, :], out_sem.at[i]).wait()
    for t in range(3):
        for copy in sent[t]:
            copy.wait_send()
    for copy in across:
        copy.wait_send()
    for t in range(3):
        low, high = bounds[t], bounds[t + 1]
        for d in range(15):
            pltpu.make_async_copy(home.at[low:high], home.at[low:high], a_send.at[t]).wait()
    for copy in tails:
        copy.wait_send()
    pltpu.make_async_copy(others, others, s1_send).wait()


def attend(table, offsets, counts, queries, keys, values, form):
    Q, R = FORMS[form]
    dma = pltpu.SemaphoreType.DMA
    return pl.pallas_call(
        functools.partial(kernel, form),
        out_shape=jax.ShapeDtypeStruct(queries.shape, BF16),
        in_specs=[
            pl.BlockSpec(memory_space=pl.ANY),
            pl.BlockSpec(memory_space=pl.ANY),
            pl.BlockSpec(memory_space=pl.ANY),
            pl.BlockSpec(memory_space=pl.ANY),
            pl.BlockSpec(memory_space=pl.ANY),
            pl.BlockSpec(memory_space=pl.ANY),
        ],
        out_specs=pl.BlockSpec(memory_space=pl.ANY),
        scratch_shapes=[
            pltpu.SMEM((8, 128), jnp.int32),
            pltpu.SMEM((SSLOTS, HEADS), jnp.int32),
            pltpu.SMEM((HEADS,), jnp.int32),
            pltpu.VMEM((256, HEADS, HDIM), BF16),
            pltpu.VMEM((256, KV_HEADS, HDIM), BF16),
            pltpu.VMEM((256, KV_HEADS, HDIM), BF16),
            pltpu.VMEM((16, BLOCK, 2 * HDIM), BF16),
            pltpu.VMEM((16, BLOCK, 2 * HDIM), BF16),
            pltpu.VMEM((R, 4, 2, BLOCK, HDIM), BF16),
            pltpu.VMEM((R, CTX, 16, HDIM), BF16),
            pltpu.VMEM((Q, 16, HDIM), BF16),
            pltpu.VMEM((2 * Q, 4, 2, 2, 4, 16, HDIM), BF16),
            pltpu.VMEM((HEADS, BLOCK, 3 * BLOCK), F32),
            pltpu.VMEM((HEADS, 256, HDIM), BF16),
            pltpu.VMEM((HEADS, 256, 2 * HDIM), F32),
            pltpu.VMEM((HEADS, 256, HDIM), F32),
            pltpu.VMEM((2, 256, 16, HDIM), BF16),
            dma((6,)),
            dma((2,)),
            dma(()),
            dma(()),
            dma((3,)),
            dma((3,)),
            dma((3, 6)),
            dma((3, 6)),
            dma((21,)),
            dma((21,)),
            dma((8,)),
            dma((8,)),
        ],
        compiler_params=pltpu.CompilerParams(
            collective_id=form, has_side_effects=True, vmem_limit_bytes=60 * 2**20
        ),
    )(table, offsets, counts, queries, keys, values)


def table_kernel(blocks_hbm, counts_hbm, o_ref, blocks, counts, column, sems):
    copies = [
        pltpu.make_async_copy(blocks_hbm, blocks, sems.at[0]),
        pltpu.make_async_copy(counts_hbm, counts, sems.at[1]),
    ]
    for copy in copies:
        copy.start()
    c = lax.axis_index("ctx")
    k = lax.axis_index("head")
    for copy in copies:
        copy.wait()
    for i in range(HEADS * VSLOTS):
        block = blocks[i % VSLOTS, i // VSLOTS]
        block = jnp.where(i % VSLOTS < counts[i // VSLOTS], block, block + 1024)
        column[pl.ds(i, 1), :] = jnp.full((1, 128), block, jnp.int32)
    shape = (128, 128)
    down, across = column[...], column[...].astype(F32).T.astype(jnp.int32)
    i, j = lax.broadcasted_iota(jnp.int32, shape, 0), lax.broadcasted_iota(jnp.int32, shape, 1)
    live_i, live_j = down < 1024, across < 1024
    pid_i = down * KV_HEADS + i // 16
    pid_j = across * KV_HEADS + j // 16
    core_i, core_j = (down // 2) % 2, (across // 2) % 2
    same = pid_i == pid_j

    def total(mask, axis):
        return jnp.sum(jnp.where(mask, 1.0, 0.0), axis=axis, keepdims=True).astype(jnp.int32)

    def wide(a):
        return jnp.broadcast_to(a, shape)

    first_i = live_i & (wide(total(same & live_j & (j < i), 1)) == 0)
    first_j = live_j & (wide(total(same & live_i & (i < j), 0)) == 0)
    rank_i = wide(total(first_j & (core_i == core_j) & (pid_j < pid_i), 1))
    rank_j = wide(total(first_i & (core_i == core_j) & (pid_i < pid_j), 0))
    load_i = wide(total(first_j & (down // 2 == across // 2), 1))
    level = 0
    for q, r in FORMS[:2]:
        bad = total(live_i & ((rank_i >= q * 4) | (load_i > r * 4)), 0)
        level = level + jnp.where(bad > 0, 1, 0)
    q0 = (c * 2 + k) * 2
    near = q0 - 2 + j % 4
    listed = total(live_i & (i // 4 == j // 4) & (down == near), 0)
    codes = jnp.where(near[:1] < 0, 2, jnp.minimum(listed, 1))
    mine = first_i & (down // 2 == c * 2 + k)
    kept = first_i & (core_i == k) & (rank_i == (j - 32) * 4 + c // 16)
    turn = jnp.where(j < 8, rank_i % 4, jnp.where(j < 16, rank_i % 8 + 8, rank_i % 16 + 16))
    hit = jnp.where(j < 32, jnp.where(mine & (turn == j), 1, 0), jnp.where(kept, 1, 0))
    value = jnp.where(j < 32, (i // 16) * 2 + down % 2, down // 4)
    rest = jnp.sum(jnp.where(hit == 1, value, 0).astype(F32), axis=0, keepdims=True)

    def seen(ahead):
        return jnp.where(across[:1] <= ahead, 1, 0)

    for form, (q, _) in enumerate(FORMS):
        place = core_j[:1] * (q * 4) + rank_j[:1]
        o_ref[form : form + 1, :] = jnp.where(across[:1] < 1024, place, 0)
    o_ref[CODE : CODE + 1, :] = codes
    o_ref[CSEE : CSEE + 1, :] = seen(q0 - 3)
    o_ref[CSEE + 1 : CSEE + 2, :] = seen(q0 - 2)
    o_ref[REST : REST + 1, :] = rest.astype(jnp.int32)
    o_ref[LEVEL : LEVEL + 1, :] = level


def tables_of(column_blocks, column_count):
    return pl.pallas_call(
        table_kernel,
        out_shape=jax.ShapeDtypeStruct((8, 128), jnp.int32),
        in_specs=[pl.BlockSpec(memory_space=pl.ANY), pl.BlockSpec(memory_space=pl.ANY)],
        out_specs=pl.BlockSpec(memory_space=pltpu.VMEM),
        scratch_shapes=[
            pltpu.SMEM((VSLOTS, HEADS), jnp.int32),
            pltpu.SMEM((HEADS,), jnp.int32),
            pltpu.VMEM((128, 128), jnp.int32),
            pltpu.SemaphoreType.DMA((2,)),
        ],
        cost_estimate=pl.CostEstimate(flops=10**6, bytes_accessed=10**5, transcendentals=0),
    )(column_blocks, column_count)


def body(queries, key_states, value_states, column_blocks, column_count, slash_offsets, slash_count):
    table = tables_of(column_blocks.T, column_count)
    offsets = slash_offsets.T

    def run(form):
        return lambda: attend(
            table, offsets, slash_count, queries, key_states, value_states, form
        )

    return lax.switch(table[LEVEL, 0], [run(form) for form in range(len(FORMS))])


def solution(mesh):
    placed = (
        P(("ctx", "head"), None, None),
        P(("ctx", "head"), None, None),
        P(("ctx", "head"), None, None),
        P(),
        P(),
        P(),
        P(),
    )
    return jax.shard_map(
        body, mesh=mesh, in_specs=placed, out_specs=P(("ctx", "head"), None, None), check_vma=False
    )
```

```python
import functools
import math

import jax
import jax.numpy as jnp
from jax import lax
from jax.experimental import pallas as pl
from jax.experimental.pallas import tpu as pltpu
from jax.sharding import PartitionSpec as P

HEADS = 32
KV_HEADS = 8
HDIM = 128
BLOCK = 128
VSLOTS = 4
SSLOTS = 16
BAND = 256
CTX = 64
SIDE = 4
NEG = -1e30
MESH = pl.DeviceIdType.MESH
BF16 = jnp.bfloat16
F32 = jnp.float32
FACTOR = 1.4426950408889634 / math.sqrt(HDIM)
NT = (((1,), (1,)), ((), ()))
CODE, CSEE, REST, LEVEL = 3, 4, 6, 7
FORMS = ((12, 1), (14, 2), (32, 4))


def kernel(
    form, t_hbm, off_hbm, cnt_hbm, q_hbm, k_hbm, v_hbm, o_hbm,
    tab, offsets, counts, qv, kin, vin, kvt, halo, send, recv, home, g_all, tables, qt, acc, tops, outs,
    in_sem, out_sem, s1_send, s1_recv, a_send, a_recv, b_send, b_recv, sib_send, sib_recv,
    halo_send, halo_recv,
):
    Q, R = FORMS[form]
    c = lax.axis_index("ctx")
    k = lax.axis_index("head")
    coords = (c // 16, (c // 4) % 4, c % 4)
    fetch = [
        pltpu.make_async_copy(k_hbm, kin, in_sem.at[0]),
        pltpu.make_async_copy(v_hbm, vin, in_sem.at[1]),
        pltpu.make_async_copy(q_hbm, qv, in_sem.at[2]),
        pltpu.make_async_copy(t_hbm, tab, in_sem.at[3]),
        pltpu.make_async_copy(off_hbm, offsets, in_sem.at[4]),
        pltpu.make_async_copy(cnt_hbm, counts, in_sem.at[5]),
    ]
    for copy in fetch:
        copy.start()
    barrier = pltpu.get_barrier_semaphore()

    @pl.loop(1, CTX)
    def _(d):
        pl.semaphore_signal(barrier, inc=1, device_id={"ctx": (c + d) % CTX}, device_id_type=MESH)

    pl.semaphore_signal(barrier, inc=1, device_id={"head": 1 - k}, device_id_type=MESH)

    @pl.when(k == 0)
    def _():
        pl.semaphore_signal(
            barrier, inc=1, device_id={"ctx": (c + CTX - 1) % CTX, "head": 1}, device_id_type=MESH
        )

    fetch[0].wait()
    fetch[1].wait()
    kt = jnp.swapaxes(kin[...], 0, 1)
    vt = jnp.swapaxes(vin[...], 0, 1)
    kvt[:, :, :HDIM] = kt.reshape(16, BLOCK, HDIM)
    kvt[:, :, HDIM:] = vt.reshape(16, BLOCK, HDIM)
    fetch[3].wait()
    for r in range(R):
        for u in range(4):
            pair = kvt[tab[REST, (0, 8, 16)[form] + r * 4 + u]]
            send[r, u, 0] = pair[:, :HDIM]
            send[r, u, 1] = pair[:, HDIM:]
    pl.semaphore_wait(barrier, CTX + k)

    @pl.loop(1, CTX)
    def _(d):
        p = (c + d) % CTX
        for r in range(R):
            pltpu.make_async_remote_copy(
                src_ref=send.at[r, p // 16, (p // 8) % 2, pl.ds((p % 8) * 16, 16)],
                dst_ref=recv.at[r, c],
                send_sem=s1_send,
                recv_sem=s1_recv,
                device_id={"ctx": p},
                device_id_type=MESH,
            ).start()

    tails = []

    def pass_on(first, last):
        for g in range(first, last):
            copy = pltpu.make_async_remote_copy(
                src_ref=kvt.at[2 * g : 2 * g + 2], dst_ref=halo.at[2 * g : 2 * g + 2],
                send_sem=halo_send.at[g], recv_sem=halo_recv.at[g],
                device_id={"ctx": (c + k) % CTX, "head": 1 - k}, device_id_type=MESH,
            )
            copy.start()
            tails.append(copy)

    pass_on(0, 4)
    for r in range(R):
        recv[r, c] = send[r, c // 16, (c // 8) % 2, pl.ds((c % 8) * 16, 16)]

    fetch[2].wait()

    for i in range(2):
        qt[i * 16 : i * 16 + 16] = jnp.swapaxes(qv[:, i * 16 : i * 16 + 16, :], 0, 1)

    fetch[4].wait()
    fetch[5].wait()
    spot = 2 * BLOCK - lax.broadcasted_iota(jnp.int32, (1, 3 * BLOCK), 1)

    @pl.loop(0, HEADS)
    def _(h):
        used = counts[h]
        line = jnp.full((1, 3 * BLOCK), NEG, F32)
        for s in range(SSLOTS):
            offset = jnp.where(s < used, offsets[s, h], -1000)
            line = jnp.where(spot == offset, 0.0, line)
        line = jnp.broadcast_to(line, (BLOCK, 3 * BLOCK))
        tables[h] = pltpu.roll(line, 0, 1, stride=1, stride_axis=0)

    row = lax.broadcasted_iota(jnp.int32, (BLOCK, BLOCK), 0)
    col = lax.broadcasted_iota(jnp.int32, (BLOCK, BLOCK), 1)
    triangle = jnp.where(col <= row, 0.0, NEG)
    ones = jnp.ones((3 * BLOCK, HDIM), BF16)

    def band(first, last):
        for g in range(first, last):
            tails[g].wait_recv()

        @pl.loop(first, last)
        def _(g):
            blocks = [halo[2 * g], halo[2 * g + 1], kvt[2 * g], kvt[2 * g + 1]]
            for j in range(2):
                window = jnp.concatenate(blocks[j : j + 3], axis=0)
                rows = qt[pl.ds(g * 4, 4), j * BLOCK : (j + 1) * BLOCK, :]
                score = lax.dot_general(
                    rows.reshape(4 * BLOCK, HDIM), window[:, :HDIM], NT, preferred_element_type=F32
                )
                weights = []
                for hh in range(4):
                    h = g * 4 + hh
                    pieces = []
                    for w in range(3):
                        code = tab[CODE, h * 4 + j + w]
                        cut = slice(w * BLOCK, (w + 1) * BLOCK)
                        plain = tables[h, :, cut]
                        if w == 2:
                            bias = jnp.where(code == 1, triangle, plain)
                        else:
                            least = jnp.where(code == 1, 0.0, NEG)
                            most = jnp.where(code == 2, NEG, 0.0)
                            bias = jnp.minimum(jnp.maximum(plain, least), most)
                        pieces.append(score[hh * BLOCK : (hh + 1) * BLOCK, cut] + bias)
                    masked = jnp.concatenate(pieces, axis=1)
                    top = jnp.max(masked, axis=1, keepdims=True)
                    weights.append(jnp.exp2((masked - top) * FACTOR).astype(BF16))
                    tops[h, pl.ds(j * BLOCK, BLOCK), :] = jnp.broadcast_to(top, (BLOCK, HDIM))
                both = jnp.concatenate([window[:, HDIM:], ones], axis=1)
                mixed = jnp.dot(
                    jnp.concatenate(weights, axis=0), both, preferred_element_type=F32
                )
                acc[pl.ds(g * 4, 4), j * BLOCK : (j + 1) * BLOCK, :] = mixed.reshape(
                    4, BLOCK, 2 * HDIM
                )

    others = recv.at[:, pl.ds(0, CTX - 1)]
    pltpu.make_async_copy(others, others, s1_recv).wait()
    for q in range(Q):
        home[q] = recv[q % R, tab[REST, 32 + q]]

    bounds = [0, (Q + 2) // 3, (2 * Q + 2) // 3, Q]

    def view(t, index, half=None):
        low, high = bounds[t], bounds[t + 1]
        middle = (low + high + 1) // 2
        if half == 0:
            high = middle
        if half == 1:
            low = middle
        x, y, z = index
        yh, yl = (slice(None), slice(None)) if y is None else (y // 2, y % 2)
        x = slice(None) if x is None else x
        z = slice(None) if z is None else z
        return g_all.at[pl.ds(k * Q + low, high - low), x, yh, yl, z]

    def moved(axis, delta, axis2=0, delta2=0):
        there = list(coords)
        there[axis] = (there[axis] + delta) % SIDE
        there[axis2] = (there[axis2] + delta2) % SIDE
        return {"ctx": there[0] * 16 + there[1] * 4 + there[2]}

    for t in range(3):
        low, high = bounds[t], bounds[t + 1]
        pltpu.make_async_copy(home.at[low:high], view(t, coords), a_recv.at[t]).start()

    for t in range(3):
        low, high = bounds[t], bounds[t + 1]

        @pl.loop(1, 16)
        def _(d):
            pltpu.make_async_remote_copy(
                src_ref=home.at[low:high], dst_ref=view(t, coords),
                send_sem=a_send.at[t], recv_sem=a_recv.at[t],
                device_id=moved(t, d // 4, (t + 1) % 3, d % 4), device_id_type=MESH,
            ).start()

    pass_on(4, 8)
    band(0, 2)

    across = []

    def to_sibling(ref):
        i = len(across)
        copy = pltpu.make_async_remote_copy(
            src_ref=ref, dst_ref=ref, send_sem=sib_send.at[i], recv_sem=sib_recv.at[i],
            device_id={"head": 1 - k}, device_id_type=MESH,
        )
        copy.start()
        across.append(copy)

    def slab(t, pos, half=None):
        index = [None, None, None]
        index[(t + 2) % 3] = pos
        return view(t, index, half)

    def push(t, pos, half, i, delta):
        ref = slab(t, pos, half)
        copy = pltpu.make_async_remote_copy(
            src_ref=ref, dst_ref=ref, send_sem=b_send.at[t, i], recv_sem=b_recv.at[t, i],
            device_id=moved((t + 2) % 3, delta), device_id_type=MESH,
        )
        copy.start()
        return copy

    sent = []
    for t in range(3):
        me = coords[(t + 2) % 3]
        whole = slab(t, me)
        pltpu.make_async_copy(whole, whole, a_recv.at[t]).wait()
        sent.append(
            [
                push(t, me, 0, 0, 1),
                push(t, me, 1, 1, -1),
                push(t, me, 1, 2, 1),
                push(t, me, 0, 3, -1),
            ]
        )
    for t in range(3):
        to_sibling(slab(t, coords[(t + 2) % 3]))
    band(2, 4)
    for t in range(3):
        me = coords[(t + 2) % 3]
        left, right = (me + 3) % 4, (me + 1) % 4
        sent[t][0].wait_recv()
        sent[t].append(push(t, left, 0, 4, 1))
        sent[t][1].wait_recv()
        sent[t].append(push(t, right, 1, 5, -1))
        to_sibling(slab(t, left, 0))
        to_sibling(slab(t, right, 1))
    band(4, 7)
    for t in range(3):
        me = coords[(t + 2) % 3]
        left, right = (me + 3) % 4, (me + 1) % 4
        sent[t][2].wait_recv()
        to_sibling(slab(t, left, 1))
        sent[t][3].wait_recv()
        to_sibling(slab(t, right, 0))
    for t in range(3):
        opposite = (coords[(t + 2) % 3] + 2) % 4
        sent[t][4].wait_recv()
        to_sibling(slab(t, opposite, 0))
        sent[t][5].wait_recv()
        to_sibling(slab(t, opposite, 1))
    band(7, 8)
    for copy in across:
        copy.wait_recv()

    ones4 = jnp.ones((VSLOTS * BLOCK, HDIM), BF16)

    def columns_of(first, last):
        @pl.loop(first, last, step=16)
        def _(base):
            def scored(h):
                keys, values = [], []
                for s in range(VSLOTS):
                    at = tab[form, h * VSLOTS + s]
                    keys.append(g_all[at // 4, at % 4, 0].reshape(BLOCK, HDIM))
                    values.append(g_all[at // 4, at % 4, 1].reshape(BLOCK, HDIM))
                keys = jnp.concatenate(keys, axis=0)
                values = jnp.concatenate(values, axis=0)
                score = lax.dot_general(qt[h], keys, NT, preferred_element_type=F32)
                return values, score

            def weighted(h, score):
                parts = []
                for j in range(2):
                    pieces = []
                    for s in range(VSLOTS):
                        see = tab[CSEE + j, h * VSLOTS + s]
                        bias = jnp.where(see == 1, 0.0, NEG)
                        pieces.append(
                            score[j * BLOCK : (j + 1) * BLOCK, s * BLOCK : (s + 1) * BLOCK] + bias
                        )
                    parts.append(jnp.concatenate(pieces, axis=1))
                masked = jnp.concatenate(parts, axis=0)
                top = tops[h]
                new = jnp.maximum(top, jnp.max(masked, axis=1, keepdims=True))
                shift = jnp.concatenate([new] * VSLOTS, axis=1)
                weights = jnp.exp2((masked - shift) * FACTOR).astype(BF16)
                return weights, jnp.exp2((top - new) * FACTOR)

            def finished(h, values, weights, keep):
                both = jnp.concatenate([values, ones4], axis=1)
                mixed = jnp.dot(weights, both, preferred_element_type=F32)
                upper = acc[h, :, :HDIM] * keep + mixed[:, :HDIM]
                lower = acc[h, :, HDIM:] * keep + mixed[:, HDIM:]
                qt[h] = (upper / lower).astype(BF16)

            ahead = scored(base)
            for i in range(16):
                h = base + i
                values, score = ahead
                if i < 15:
                    ahead = scored(h + 1)
                finished(h, values, *weighted(h, score))

    for i in range(2):
        sixteen = slice(i * 16, i * 16 + 16)
        columns_of(i * 16, i * 16 + 16)
        outs[i] = jnp.swapaxes(qt[sixteen], 0, 1)
        pltpu.make_async_copy(outs.at[i], o_hbm.at[:, sixteen, :], out_sem.at[i]).start()
    for i in range(2):
        sixteen = slice(i * 16, i * 16 + 16)
        pltpu.make_async_copy(outs.at[i], o_hbm.at[:, sixteen, :], out_sem.at[i]).wait()
    for t in range(3):
        for copy in sent[t]:
            copy.wait_send()
    for copy in across:
        copy.wait_send()
    for t in range(3):
        low, high = bounds[t], bounds[t + 1]
        for d in range(15):
            pltpu.make_async_copy(home.at[low:high], home.at[low:high], a_send.at[t]).wait()
    for copy in tails:
        copy.wait_send()
    pltpu.make_async_copy(others, others, s1_send).wait()


def attend(table, offsets, counts, queries, keys, values, form):
    Q, R = FORMS[form]
    dma = pltpu.SemaphoreType.DMA
    return pl.pallas_call(
        functools.partial(kernel, form),
        out_shape=jax.ShapeDtypeStruct(queries.shape, BF16),
        in_specs=[
            pl.BlockSpec(memory_space=pl.ANY),
            pl.BlockSpec(memory_space=pl.ANY),
            pl.BlockSpec(memory_space=pl.ANY),
            pl.BlockSpec(memory_space=pl.ANY),
            pl.BlockSpec(memory_space=pl.ANY),
            pl.BlockSpec(memory_space=pl.ANY),
        ],
        out_specs=pl.BlockSpec(memory_space=pl.ANY),
        scratch_shapes=[
            pltpu.SMEM((8, 128), jnp.int32),
            pltpu.SMEM((SSLOTS, HEADS), jnp.int32),
            pltpu.SMEM((HEADS,), jnp.int32),
            pltpu.VMEM((256, HEADS, HDIM), BF16),
            pltpu.VMEM((256, KV_HEADS, HDIM), BF16),
            pltpu.VMEM((256, KV_HEADS, HDIM), BF16),
            pltpu.VMEM((16, BLOCK, 2 * HDIM), BF16),
            pltpu.VMEM((16, BLOCK, 2 * HDIM), BF16),
            pltpu.VMEM((R, 4, 2, BLOCK, HDIM), BF16),
            pltpu.VMEM((R, CTX, 16, HDIM), BF16),
            pltpu.VMEM((Q, 16, HDIM), BF16),
            pltpu.VMEM((2 * Q, 4, 2, 2, 4, 16, HDIM), BF16),
            pltpu.VMEM((HEADS, BLOCK, 3 * BLOCK), F32),
            pltpu.VMEM((HEADS, 256, HDIM), BF16),
            pltpu.VMEM((HEADS, 256, 2 * HDIM), F32),
            pltpu.VMEM((HEADS, 256, HDIM), F32),
            pltpu.VMEM((2, 256, 16, HDIM), BF16),
            dma((6,)),
            dma((2,)),
            dma(()),
            dma(()),
            dma((3,)),
            dma((3,)),
            dma((3, 6)),
            dma((3, 6)),
            dma((21,)),
            dma((21,)),
            dma((8,)),
            dma((8,)),
        ],
        compiler_params=pltpu.CompilerParams(
            collective_id=form, has_side_effects=True, vmem_limit_bytes=60 * 2**20
        ),
    )(table, offsets, counts, queries, keys, values)


def table_kernel(blocks_hbm, counts_hbm, o_ref, blocks, counts, column, sems):
    copies = [
        pltpu.make_async_copy(blocks_hbm, blocks, sems.at[0]),
        pltpu.make_async_copy(counts_hbm, counts, sems.at[1]),
    ]
    for copy in copies:
        copy.start()
    c = lax.axis_index("ctx")
    k = lax.axis_index("head")
    for copy in copies:
        copy.wait()
    for i in range(HEADS * VSLOTS):
        block = blocks[i % VSLOTS, i // VSLOTS]
        block = jnp.where(i % VSLOTS < counts[i // VSLOTS], block, block + 1024)
        column[pl.ds(i, 1), :] = jnp.full((1, 128), block, jnp.int32)
    shape = (128, 128)
    down, across = column[...], column[...].astype(F32).T.astype(jnp.int32)
    i, j = lax.broadcasted_iota(jnp.int32, shape, 0), lax.broadcasted_iota(jnp.int32, shape, 1)
    live_i, live_j = down < 1024, across < 1024
    pid_i = down * KV_HEADS + i // 16
    pid_j = across * KV_HEADS + j // 16
    core_i, core_j = (down // 2) % 2, (across // 2) % 2
    same = pid_i == pid_j

    def total(mask, axis):
        return jnp.sum(jnp.where(mask, 1.0, 0.0), axis=axis, keepdims=True).astype(jnp.int32)

    def wide(a):
        return jnp.broadcast_to(a, shape)

    first_i = live_i & (wide(total(same & live_j & (j < i), 1)) == 0)
    first_j = live_j & (wide(total(same & live_i & (i < j), 0)) == 0)
    rank_i = wide(total(first_j & (core_i == core_j) & (pid_j < pid_i), 1))
    rank_j = wide(total(first_i & (core_i == core_j) & (pid_i < pid_j), 0))
    load_i = wide(total(first_j & (down // 2 == across // 2), 1))
    level = 0
    for q, r in FORMS[:2]:
        bad = total(live_i & ((rank_i >= q * 4) | (load_i > r * 4)), 0)
        level = level + jnp.where(bad > 0, 1, 0)
    q0 = (c * 2 + k) * 2
    near = q0 - 2 + j % 4
    listed = total(live_i & (i // 4 == j // 4) & (down == near), 0)
    codes = jnp.where(near[:1] < 0, 2, jnp.minimum(listed, 1))
    mine = first_i & (down // 2 == c * 2 + k)
    kept = first_i & (core_i == k) & (rank_i == (j - 32) * 4 + c // 16)
    turn = jnp.where(j < 8, rank_i % 4, jnp.where(j < 16, rank_i % 8 + 8, rank_i % 16 + 16))
    hit = jnp.where(j < 32, jnp.where(mine & (turn == j), 1, 0), jnp.where(kept, 1, 0))
    value = jnp.where(j < 32, (i // 16) * 2 + down % 2, down // 4)
    rest = jnp.sum(jnp.where(hit == 1, value, 0).astype(F32), axis=0, keepdims=True)

    def seen(ahead):
        return jnp.where(across[:1] <= ahead, 1, 0)

    for form, (q, _) in enumerate(FORMS):
        place = core_j[:1] * (q * 4) + rank_j[:1]
        o_ref[form : form + 1, :] = jnp.where(across[:1] < 1024, place, 0)
    o_ref[CODE : CODE + 1, :] = codes
    o_ref[CSEE : CSEE + 1, :] = seen(q0 - 3)
    o_ref[CSEE + 1 : CSEE + 2, :] = seen(q0 - 2)
    o_ref[REST : REST + 1, :] = rest.astype(jnp.int32)
    o_ref[LEVEL : LEVEL + 1, :] = level


def tables_of(column_blocks, column_count):
    return pl.pallas_call(
        table_kernel,
        out_shape=jax.ShapeDtypeStruct((8, 128), jnp.int32),
        in_specs=[pl.BlockSpec(memory_space=pl.ANY), pl.BlockSpec(memory_space=pl.ANY)],
        out_specs=pl.BlockSpec(memory_space=pltpu.VMEM),
        scratch_shapes=[
            pltpu.SMEM((VSLOTS, HEADS), jnp.int32),
            pltpu.SMEM((HEADS,), jnp.int32),
            pltpu.VMEM((128, 128), jnp.int32),
            pltpu.SemaphoreType.DMA((2,)),
        ],
        cost_estimate=pl.CostEstimate(flops=10**6, bytes_accessed=10**5, transcendentals=0),
    )(column_blocks, column_count)


def body(queries, key_states, value_states, column_blocks, column_count, slash_offsets, slash_count):
    table = tables_of(column_blocks.T, column_count)
    offsets = slash_offsets.T

    def run(form):
        return lambda: attend(
            table, offsets, slash_count, queries, key_states, value_states, form
        )

    return lax.switch(table[LEVEL, 0], [run(form) for form in range(len(FORMS))])


def solution(mesh):
    placed = (
        P(("ctx", "head"), None, None),
        P(("ctx", "head"), None, None),
        P(("ctx", "head"), None, None),
        P(),
        P(),
        P(),
        P(),
    )
    return jax.shard_map(
        body, mesh=mesh, in_specs=placed, out_specs=P(("ctx", "head"), None, None), check_vma=False
    )
```

```python
import functools
import math

import jax
import jax.numpy as jnp
from jax import lax
from jax.experimental import pallas as pl
from jax.experimental.pallas import tpu as pltpu
from jax.sharding import PartitionSpec as P

HEADS = 32
KV_HEADS = 8
HDIM = 128
BLOCK = 128
VSLOTS = 4
SSLOTS = 16
BAND = 256
CTX = 64
SIDE = 4
NEG = -1e30
MESH = pl.DeviceIdType.MESH
BF16 = jnp.bfloat16
F32 = jnp.float32
FACTOR = 1.4426950408889634 / math.sqrt(HDIM)
NT = (((1,), (1,)), ((), ()))
CODE, CSEE, REST, LEVEL = 3, 4, 6, 7
FORMS = ((14, 1), (16, 2), (32, 4))


def kernel(
    form, t_hbm, off_hbm, cnt_hbm, q_hbm, k_hbm, v_hbm, o_hbm,
    tab, offsets, counts, qv, kin, vin, kvt, halo, send, recv, home, g_all, tables, qt, acc, tops, outs,
    in_sem, out_sem, s1_send, s1_recv, a_send, a_recv, b_send, b_recv, sib_send, sib_recv,
    halo_send, halo_recv,
):
    Q, R = FORMS[form]
    c = lax.axis_index("ctx")
    k = lax.axis_index("head")
    coords = (c // 16, (c // 4) % 4, c % 4)
    fetch = [
        pltpu.make_async_copy(k_hbm, kin, in_sem.at[0]),
        pltpu.make_async_copy(v_hbm, vin, in_sem.at[1]),
        pltpu.make_async_copy(q_hbm, qv, in_sem.at[2]),
        pltpu.make_async_copy(t_hbm, tab, in_sem.at[3]),
        pltpu.make_async_copy(off_hbm, offsets, in_sem.at[4]),
        pltpu.make_async_copy(cnt_hbm, counts, in_sem.at[5]),
    ]
    for copy in fetch:
        copy.start()
    barrier = pltpu.get_barrier_semaphore()

    @pl.loop(1, CTX)
    def _(d):
        pl.semaphore_signal(barrier, inc=1, device_id={"ctx": (c + d) % CTX}, device_id_type=MESH)

    pl.semaphore_signal(barrier, inc=1, device_id={"head": 1 - k}, device_id_type=MESH)

    @pl.when(k == 0)
    def _():
        pl.semaphore_signal(
            barrier, inc=1, device_id={"ctx": (c + CTX - 1) % CTX, "head": 1}, device_id_type=MESH
        )

    fetch[0].wait()
    fetch[1].wait()
    kt = jnp.swapaxes(kin[...], 0, 1)
    vt = jnp.swapaxes(vin[...], 0, 1)
    kvt[:, :, :HDIM] = kt.reshape(16, BLOCK, HDIM)
    kvt[:, :, HDIM:] = vt.reshape(16, BLOCK, HDIM)
    fetch[3].wait()
    for r in range(R):
        for u in range(4):
            pair = kvt[tab[REST, (0, 8, 16)[form] + r * 4 + u]]
            send[r, u, 0] = pair[:, :HDIM]
            send[r, u, 1] = pair[:, HDIM:]
    pl.semaphore_wait(barrier, CTX + k)

    @pl.loop(1, CTX)
    def _(d):
        p = (c + d) % CTX
        for r in range(R):
            pltpu.make_async_remote_copy(
                src_ref=send.at[r, p // 16, (p // 8) % 2, pl.ds((p % 8) * 16, 16)],
                dst_ref=recv.at[r, c],
                send_sem=s1_send,
                recv_sem=s1_recv,
                device_id={"ctx": p},
                device_id_type=MESH,
            ).start()

    tails = []

    def pass_on(first, last):
        for g in range(first, last):
            copy = pltpu.make_async_remote_copy(
                src_ref=kvt.at[2 * g : 2 * g + 2], dst_ref=halo.at[2 * g : 2 * g + 2],
                send_sem=halo_send.at[g], recv_sem=halo_recv.at[g],
                device_id={"ctx": (c + k) % CTX, "head": 1 - k}, device_id_type=MESH,
            )
            copy.start()
            tails.append(copy)

    pass_on(0, 4)
    for r in range(R):
        recv[r, c] = send[r, c // 16, (c // 8) % 2, pl.ds((c % 8) * 16, 16)]

    fetch[2].wait()

    for i in range(2):
        qt[i * 16 : i * 16 + 16] = jnp.swapaxes(qv[:, i * 16 : i * 16 + 16, :], 0, 1)

    fetch[4].wait()
    fetch[5].wait()
    spot = 2 * BLOCK - lax.broadcasted_iota(jnp.int32, (1, 3 * BLOCK), 1)

    @pl.loop(0, HEADS)
    def _(h):
        used = counts[h]
        line = jnp.full((1, 3 * BLOCK), NEG, F32)
        for s in range(SSLOTS):
            offset = jnp.where(s < used, offsets[s, h], -1000)
            line = jnp.where(spot == offset, 0.0, line)
        line = jnp.broadcast_to(line, (BLOCK, 3 * BLOCK))
        tables[h] = pltpu.roll(line, 0, 1, stride=1, stride_axis=0)

    row = lax.broadcasted_iota(jnp.int32, (BLOCK, BLOCK), 0)
    col = lax.broadcasted_iota(jnp.int32, (BLOCK, BLOCK), 1)
    triangle = jnp.where(col <= row, 0.0, NEG)
    ones = jnp.ones((3 * BLOCK, HDIM), BF16)

    def band(first, last):
        for g in range(first, last):
            tails[g].wait_recv()

        @pl.loop(first, last)
        def _(g):
            blocks = [halo[2 * g], halo[2 * g + 1], kvt[2 * g], kvt[2 * g + 1]]
            for j in range(2):
                window = jnp.concatenate(blocks[j : j + 3], axis=0)
                rows = qt[pl.ds(g * 4, 4), j * BLOCK : (j + 1) * BLOCK, :]
                score = lax.dot_general(
                    rows.reshape(4 * BLOCK, HDIM), window[:, :HDIM], NT, preferred_element_type=F32
                )
                weights = []
                for hh in range(4):
                    h = g * 4 + hh
                    pieces = []
                    for w in range(3):
                        code = tab[CODE, h * 4 + j + w]
                        cut = slice(w * BLOCK, (w + 1) * BLOCK)
                        plain = tables[h, :, cut]
                        if w == 2:
                            bias = jnp.where(code == 1, triangle, plain)
                        else:
                            least = jnp.where(code == 1, 0.0, NEG)
                            most = jnp.where(code == 2, NEG, 0.0)
                            bias = jnp.minimum(jnp.maximum(plain, least), most)
                        pieces.append(score[hh * BLOCK : (hh + 1) * BLOCK, cut] + bias)
                    masked = jnp.concatenate(pieces, axis=1)
                    top = jnp.max(masked, axis=1, keepdims=True)
                    weights.append(jnp.exp2((masked - top) * FACTOR).astype(BF16))
                    tops[h, pl.ds(j * BLOCK, BLOCK), :] = jnp.broadcast_to(top, (BLOCK, HDIM))
                both = jnp.concatenate([window[:, HDIM:], ones], axis=1)
                mixed = jnp.dot(
                    jnp.concatenate(weights, axis=0), both, preferred_element_type=F32
                )
                acc[pl.ds(g * 4, 4), j * BLOCK : (j + 1) * BLOCK, :] = mixed.reshape(
                    4, BLOCK, 2 * HDIM
                )

    others = recv.at[:, pl.ds(0, CTX - 1)]
    pltpu.make_async_copy(others, others, s1_recv).wait()
    for q in range(Q):
        home[q] = recv[q % R, tab[REST, 32 + q]]

    bounds = [0, (Q + 2) // 3, (2 * Q + 2) // 3, Q]

    def view(t, index, half=None):
        low, high = bounds[t], bounds[t + 1]
        middle = (low + high + 1) // 2
        if half == 0:
            high = middle
        if half == 1:
            low = middle
        x, y, z = index
        yh, yl = (slice(None), slice(None)) if y is None else (y // 2, y % 2)
        x = slice(None) if x is None else x
        z = slice(None) if z is None else z
        return g_all.at[pl.ds(k * Q + low, high - low), x, yh, yl, z]

    def moved(axis, delta, axis2=0, delta2=0):
        there = list(coords)
        there[axis] = (there[axis] + delta) % SIDE
        there[axis2] = (there[axis2] + delta2) % SIDE
        return {"ctx": there[0] * 16 + there[1] * 4 + there[2]}

    for t in range(3):
        low, high = bounds[t], bounds[t + 1]
        pltpu.make_async_copy(home.at[low:high], view(t, coords), a_recv.at[t]).start()

    for t in range(3):
        low, high = bounds[t], bounds[t + 1]

        @pl.loop(1, 16)
        def _(d):
            pltpu.make_async_remote_copy(
                src_ref=home.at[low:high], dst_ref=view(t, coords),
                send_sem=a_send.at[t], recv_sem=a_recv.at[t],
                device_id=moved(t, d // 4, (t + 1) % 3, d % 4), device_id_type=MESH,
            ).start()

    pass_on(4, 8)
    band(0, 2)

    across = []

    def to_sibling(ref):
        i = len(across)
        copy = pltpu.make_async_remote_copy(
            src_ref=ref, dst_ref=ref, send_sem=sib_send.at[i], recv_sem=sib_recv.at[i],
            device_id={"head": 1 - k}, device_id_type=MESH,
        )
        copy.start()
        across.append(copy)

    def slab(t, pos, half=None):
        index = [None, None, None]
        index[(t + 2) % 3] = pos
        return view(t, index, half)

    def push(t, pos, half, i, delta):
        ref = slab(t, pos, half)
        copy = pltpu.make_async_remote_copy(
            src_ref=ref, dst_ref=ref, send_sem=b_send.at[t, i], recv_sem=b_recv.at[t, i],
            device_id=moved((t + 2) % 3, delta), device_id_type=MESH,
        )
        copy.start()
        return copy

    sent = []
    for t in range(3):
        me = coords[(t + 2) % 3]
        whole = slab(t, me)
        pltpu.make_async_copy(whole, whole, a_recv.at[t]).wait()
        sent.append(
            [
                push(t, me, 0, 0, 1),
                push(t, me, 1, 1, -1),
                push(t, me, 1, 2, 1),
                push(t, me, 0, 3, -1),
            ]
        )
    for t in range(3):
        to_sibling(slab(t, coords[(t + 2) % 3]))
    band(2, 4)
    for t in range(3):
        me = coords[(t + 2) % 3]
        left, right = (me + 3) % 4, (me + 1) % 4
        sent[t][0].wait_recv()
        sent[t].append(push(t, left, 0, 4, 1))
        sent[t][1].wait_recv()
        sent[t].append(push(t, right, 1, 5, -1))
        to_sibling(slab(t, left, 0))
        to_sibling(slab(t, right, 1))
    band(4, 7)
    for t in range(3):
        me = coords[(t + 2) % 3]
        left, right = (me + 3) % 4, (me + 1) % 4
        sent[t][2].wait_recv()
        to_sibling(slab(t, left, 1))
        sent[t][3].wait_recv()
        to_sibling(slab(t, right, 0))
    for t in range(3):
        opposite = (coords[(t + 2) % 3] + 2) % 4
        sent[t][4].wait_recv()
        to_sibling(slab(t, opposite, 0))
        sent[t][5].wait_recv()
        to_sibling(slab(t, opposite, 1))
    band(7, 8)
    for copy in across:
        copy.wait_recv()

    ones4 = jnp.ones((VSLOTS * BLOCK, HDIM), BF16)

    def columns_of(first, last):
        @pl.loop(first, last, step=16)
        def _(base):
            def scored(h):
                keys, values = [], []
                for s in range(VSLOTS):
                    at = tab[form, h * VSLOTS + s]
                    keys.append(g_all[at // 4, at % 4, 0].reshape(BLOCK, HDIM))
                    values.append(g_all[at // 4, at % 4, 1].reshape(BLOCK, HDIM))
                keys = jnp.concatenate(keys, axis=0)
                values = jnp.concatenate(values, axis=0)
                score = lax.dot_general(qt[h], keys, NT, preferred_element_type=F32)
                return values, score

            def weighted(h, score):
                parts = []
                for j in range(2):
                    pieces = []
                    for s in range(VSLOTS):
                        see = tab[CSEE + j, h * VSLOTS + s]
                        bias = jnp.where(see == 1, 0.0, NEG)
                        pieces.append(
                            score[j * BLOCK : (j + 1) * BLOCK, s * BLOCK : (s + 1) * BLOCK] + bias
                        )
                    parts.append(jnp.concatenate(pieces, axis=1))
                masked = jnp.concatenate(parts, axis=0)
                top = tops[h]
                new = jnp.maximum(top, jnp.max(masked, axis=1, keepdims=True))
                shift = jnp.concatenate([new] * VSLOTS, axis=1)
                weights = jnp.exp2((masked - shift) * FACTOR).astype(BF16)
                return weights, jnp.exp2((top - new) * FACTOR)

            def finished(h, values, weights, keep):
                both = jnp.concatenate([values, ones4], axis=1)
                mixed = jnp.dot(weights, both, preferred_element_type=F32)
                upper = acc[h, :, :HDIM] * keep + mixed[:, :HDIM]
                lower = acc[h, :, HDIM:] * keep + mixed[:, HDIM:]
                qt[h] = (upper / lower).astype(BF16)

            ahead = scored(base)
            for i in range(16):
                h = base + i
                values, score = ahead
                if i < 15:
                    ahead = scored(h + 1)
                finished(h, values, *weighted(h, score))

    for i in range(2):
        sixteen = slice(i * 16, i * 16 + 16)
        columns_of(i * 16, i * 16 + 16)
        outs[i] = jnp.swapaxes(qt[sixteen], 0, 1)
        pltpu.make_async_copy(outs.at[i], o_hbm.at[:, sixteen, :], out_sem.at[i]).start()
    for i in range(2):
        sixteen = slice(i * 16, i * 16 + 16)
        pltpu.make_async_copy(outs.at[i], o_hbm.at[:, sixteen, :], out_sem.at[i]).wait()
    for t in range(3):
        for copy in sent[t]:
            copy.wait_send()
    for copy in across:
        copy.wait_send()
    for t in range(3):
        low, high = bounds[t], bounds[t + 1]
        for d in range(15):
            pltpu.make_async_copy(home.at[low:high], home.at[low:high], a_send.at[t]).wait()
    for copy in tails:
        copy.wait_send()
    pltpu.make_async_copy(others, others, s1_send).wait()


def attend(table, offsets, counts, queries, keys, values, form):
    Q, R = FORMS[form]
    dma = pltpu.SemaphoreType.DMA
    return pl.pallas_call(
        functools.partial(kernel, form),
        out_shape=jax.ShapeDtypeStruct(queries.shape, BF16),
        in_specs=[
            pl.BlockSpec(memory_space=pl.ANY),
            pl.BlockSpec(memory_space=pl.ANY),
            pl.BlockSpec(memory_space=pl.ANY),
            pl.BlockSpec(memory_space=pl.ANY),
            pl.BlockSpec(memory_space=pl.ANY),
            pl.BlockSpec(memory_space=pl.ANY),
        ],
        out_specs=pl.BlockSpec(memory_space=pl.ANY),
        scratch_shapes=[
            pltpu.SMEM((8, 128), jnp.int32),
            pltpu.SMEM((SSLOTS, HEADS), jnp.int32),
            pltpu.SMEM((HEADS,), jnp.int32),
            pltpu.VMEM((256, HEADS, HDIM), BF16),
            pltpu.VMEM((256, KV_HEADS, HDIM), BF16),
            pltpu.VMEM((256, KV_HEADS, HDIM), BF16),
            pltpu.VMEM((16, BLOCK, 2 * HDIM), BF16),
            pltpu.VMEM((16, BLOCK, 2 * HDIM), BF16),
            pltpu.VMEM((R, 4, 2, BLOCK, HDIM), BF16),
            pltpu.VMEM((R, CTX, 16, HDIM), BF16),
            pltpu.VMEM((Q, 16, HDIM), BF16),
            pltpu.VMEM((2 * Q, 4, 2, 2, 4, 16, HDIM), BF16),
            pltpu.VMEM((HEADS, BLOCK, 3 * BLOCK), F32),
            pltpu.VMEM((HEADS, 256, HDIM), BF16),
            pltpu.VMEM((HEADS, 256, 2 * HDIM), F32),
            pltpu.VMEM((HEADS, 256, HDIM), F32),
            pltpu.VMEM((2, 256, 16, HDIM), BF16),
            dma((6,)),
            dma((2,)),
            dma(()),
            dma(()),
            dma((3,)),
            dma((3,)),
            dma((3, 6)),
            dma((3, 6)),
            dma((21,)),
            dma((21,)),
            dma((8,)),
            dma((8,)),
        ],
        compiler_params=pltpu.CompilerParams(
            collective_id=form, has_side_effects=True, vmem_limit_bytes=60 * 2**20
        ),
    )(table, offsets, counts, queries, keys, values)


def table_kernel(blocks_hbm, counts_hbm, o_ref, blocks, counts, column, sems):
    copies = [
        pltpu.make_async_copy(blocks_hbm, blocks, sems.at[0]),
        pltpu.make_async_copy(counts_hbm, counts, sems.at[1]),
    ]
    for copy in copies:
        copy.start()
    c = lax.axis_index("ctx")
    k = lax.axis_index("head")
    for copy in copies:
        copy.wait()
    for i in range(HEADS * VSLOTS):
        block = blocks[i % VSLOTS, i // VSLOTS]
        block = jnp.where(i % VSLOTS < counts[i // VSLOTS], block, block + 1024)
        column[pl.ds(i, 1), :] = jnp.full((1, 128), block, jnp.int32)
    shape = (128, 128)
    down, across = column[...], column[...].astype(F32).T.astype(jnp.int32)
    i, j = lax.broadcasted_iota(jnp.int32, shape, 0), lax.broadcasted_iota(jnp.int32, shape, 1)
    live_i, live_j = down < 1024, across < 1024
    pid_i = down * KV_HEADS + i // 16
    pid_j = across * KV_HEADS + j // 16
    core_i, core_j = (down // 2) % 2, (across // 2) % 2
    same = pid_i == pid_j

    def total(mask, axis):
        return jnp.sum(jnp.where(mask, 1.0, 0.0), axis=axis, keepdims=True).astype(jnp.int32)

    def wide(a):
        return jnp.broadcast_to(a, shape)

    first_i = live_i & (wide(total(same & live_j & (j < i), 1)) == 0)
    first_j = live_j & (wide(total(same & live_i & (i < j), 0)) == 0)
    rank_i = wide(total(first_j & (core_i == core_j) & (pid_j < pid_i), 1))
    rank_j = wide(total(first_i & (core_i == core_j) & (pid_i < pid_j), 0))
    load_i = wide(total(first_j & (down // 2 == across // 2), 1))
    level = 0
    for q, r in FORMS[:2]:
        bad = total(live_i & ((rank_i >= q * 4) | (load_i > r * 4)), 0)
        level = level + jnp.where(bad > 0, 1, 0)
    q0 = (c * 2 + k) * 2
    near = q0 - 2 + j % 4
    listed = total(live_i & (i // 4 == j // 4) & (down == near), 0)
    codes = jnp.where(near[:1] < 0, 2, jnp.minimum(listed, 1))
    mine = first_i & (down // 2 == c * 2 + k)
    kept = first_i & (core_i == k) & (rank_i == (j - 32) * 4 + c // 16)
    turn = jnp.where(j < 8, rank_i % 4, jnp.where(j < 16, rank_i % 8 + 8, rank_i % 16 + 16))
    hit = jnp.where(j < 32, jnp.where(mine & (turn == j), 1, 0), jnp.where(kept, 1, 0))
    value = jnp.where(j < 32, (i // 16) * 2 + down % 2, down // 4)
    rest = jnp.sum(jnp.where(hit == 1, value, 0).astype(F32), axis=0, keepdims=True)

    def seen(ahead):
        return jnp.where(across[:1] <= ahead, 1, 0)

    for form, (q, _) in enumerate(FORMS):
        place = core_j[:1] * (q * 4) + rank_j[:1]
        o_ref[form : form + 1, :] = jnp.where(across[:1] < 1024, place, 0)
    o_ref[CODE : CODE + 1, :] = codes
    o_ref[CSEE : CSEE + 1, :] = seen(q0 - 3)
    o_ref[CSEE + 1 : CSEE + 2, :] = seen(q0 - 2)
    o_ref[REST : REST + 1, :] = rest.astype(jnp.int32)
    o_ref[LEVEL : LEVEL + 1, :] = level


def tables_of(column_blocks, column_count):
    return pl.pallas_call(
        table_kernel,
        out_shape=jax.ShapeDtypeStruct((8, 128), jnp.int32),
        in_specs=[pl.BlockSpec(memory_space=pl.ANY), pl.BlockSpec(memory_space=pl.ANY)],
        out_specs=pl.BlockSpec(memory_space=pltpu.VMEM),
        scratch_shapes=[
            pltpu.SMEM((VSLOTS, HEADS), jnp.int32),
            pltpu.SMEM((HEADS,), jnp.int32),
            pltpu.VMEM((128, 128), jnp.int32),
            pltpu.SemaphoreType.DMA((2,)),
        ],
        cost_estimate=pl.CostEstimate(flops=10**6, bytes_accessed=10**5, transcendentals=0),
    )(column_blocks, column_count)


def body(queries, key_states, value_states, column_blocks, column_count, slash_offsets, slash_count):
    table = tables_of(column_blocks.T, column_count)
    offsets = slash_offsets.T

    def run(form):
        return lambda: attend(
            table, offsets, slash_count, queries, key_states, value_states, form
        )

    return lax.switch(table[LEVEL, 0], [run(form) for form in range(len(FORMS))])


def solution(mesh):
    placed = (
        P(("ctx", "head"), None, None),
        P(("ctx", "head"), None, None),
        P(("ctx", "head"), None, None),
        P(),
        P(),
        P(),
        P(),
    )
    return jax.shard_map(
        body, mesh=mesh, in_specs=placed, out_specs=P(("ctx", "head"), None, None), check_vma=False
    )
```
